256 devices in a mesh: seq: 16 (over z, y_hi), head: 8 (over x, core), dp: 2 (over y_lo).
Axes of the slice: x: 4, y: 4 (y_hi: 2, y_lo: 2; y = y_hi * 2 + y_lo), z: 8, core: 2. Of those that a mesh axis runs over, the one named last changes fastest.
Arguments:
- query_proj: bfloat16 [8192, 3072], P(('dp', 'seq'), 'head'), parts along dimension 0, may hold values from -12.5 to 12.5
- query_tangent: bfloat16 [8192, 3072], P(('dp', 'seq'), 'head'), parts along dimension 0, may hold values from -6 to 6
- key_proj: bfloat16 [8192, 3072], P(('dp', 'seq'), 'head'), parts along dimension 0, may hold values from -5 to 5
- key_tangent: bfloat16 [8192, 3072], P(('dp', 'seq'), 'head'), parts along dimension 0, may hold values from -5 to 5
- value_proj: bfloat16 [8192, 3072], P(('dp', 'seq'), 'head'), parts along dimension 0, may hold values from -6 to 6
- value_tangent: bfloat16 [8192, 3072], P(('dp', 'seq'), 'head'), parts along dimension 0, may hold values from -6 to 6
- residual: bfloat16 [8192, 6144], P(('dp', 'seq'), 'head'), parts along dimension 0, may hold values from -6 to 6
- residual_tangent: bfloat16 [8192, 6144], P(('dp', 'seq'), 'head'), parts along dimension 0, may hold values from -6 to 6
- out_weight: bfloat16 [3072, 6144], P('head'), may hold values from -0.15625 to 0.15625
- out_gate: float32 [12288], P(('dp', 'head')), parts along dimension 0, may hold values from 0.5 to 1.5
- out_gate_tangent: float32 [12288], P(('dp', 'head')), parts along dimension 0, may hold values from -3 to 3
Outputs:
- block_out: bfloat16 [8192, 6144], P(('dp', 'seq'), 'head'), parts along dimension 0
- block_tangent: bfloat16 [8192, 6144], P(('dp', 'seq'), 'head'), parts along dimension 0
The draws below stay inside these ranges and needn't reach their ends.
There are 2 independent parts, one for each index of `dp`. The reference program is written for one: setup_inputs(seed, part) draws one part's arguments, and reference() takes and returns one part's arrays. A program takes and returns all parts, laid end to end along the dimension named above; an argument that names none is the same for every part. Nothing has to cross between parts.
All inputs are finite; a program needn't handle non-finite values.
Results may differ from the reference program's by a relative error of at most 0.015.
Values may be sent and summed in bfloat16 or wider, within the bound.
No kernel may reach another device: no remote copies, remote signals or barrier semaphores. Data moves between devices by JAX's collectives and lax.ppermute only.
A program may use at most 64 MiB of HBM per device.

```python
import jax
import jax.numpy as jnp
from jax import lax

D = 6144
HEADS = 24
HD = 128
TOKENS = 4096
N_HEAD = 8


def shared_keys(key):
    return jnp.clip(jax.random.normal(key, (TOKENS, HEADS * HD), jnp.float32), -5.0, 5.0)


def draw_key_proj(key, part):
    base = shared_keys(key)
    values = base
    return values.astype(jnp.bfloat16)


def draw_query_proj(key, part):
    key = jax.random.fold_in(key, 5)
    values = 2.5 * jnp.clip(jax.random.normal(key, (TOKENS, HEADS * HD), jnp.float32), -5.0, 5.0)
    return values.astype(jnp.bfloat16)


def draw_key_tangent(key, part):
    key = jax.random.fold_in(key, 7)
    values = jnp.clip(jax.random.normal(key, (TOKENS, HEADS * HD), jnp.float32), -5.0, 5.0)
    return values.astype(jnp.bfloat16)


def spiked(result, stream_key, source, target, parts, factor):
    def block_of(axis_at):
        return (jnp.arange(result.shape[axis_at]) // (result.shape[axis_at] // parts)).reshape((-1,) + (1,) * (result.ndim - 1 - axis_at))

    near = jax.random.permutation(stream_key, parts)[block_of(target)]
    far = (block_of(target) + parts // 2) % parts
    return jnp.where((block_of(source) == near) | (block_of(source) == far), factor * result, result)


def block_levels(own_key, extent, cuts, low, top_value):
    def one(axis_at, blocks):
        heights = jax.random.uniform(jax.random.fold_in(jax.random.fold_in(own_key, 6), axis_at), (blocks,), jnp.float32, low / len(cuts), top_value / len(cuts))
        return jnp.repeat(jnp.exp(heights), extent[axis_at] // blocks).reshape((-1,) + (1,) * (len(extent) - axis_at - 1))

    loudness = one(*cuts[0])
    for cut in cuts[1:]:
        loudness = loudness * one(*cut)
    return loudness


def bell_draw(key, shape, width, bound, split=(), kind=jnp.bfloat16):
    drawn = jax.random.normal(key, shape, jnp.float32) * width
    if len(split) > 0:
        drawn = block_levels(key, shape, split, -0.22, 0.18) * drawn
    return jnp.clip(drawn, min=-bound, max=bound).astype(kind)


def bell_draw_with(stream_key, dims, scale, reach, shards, heavy, kind=jnp.bfloat16):
    values = scale * jax.random.normal(stream_key, dims, jnp.float32)
    if shards:
        values = values * block_levels(stream_key, dims, shards, -0.22, 0.18)
    return jnp.clip(spiked(values, jax.random.fold_in(stream_key, 3), *heavy), -reach, reach).astype(kind)


def setup_inputs(seed: int = 0, part: int = 0) -> dict:
    key_of = jax.random.split(jax.random.key(seed), 12)
    part_splits = jax.random.split(jax.random.fold_in(key_of[11], part), 12)
    query_proj = draw_query_proj(jax.random.fold_in(jax.random.fold_in(key_of[11], part), 71), part)
    query_tangent = bell_draw(part_splits[1], (TOKENS, HEADS * HD), 1.0, 6.0, ((0, 16), (1, 8)))
    key_proj = draw_key_proj(jax.random.fold_in(jax.random.fold_in(key_of[11], part), 71), part)
    key_tangent = draw_key_tangent(jax.random.fold_in(jax.random.fold_in(key_of[11], part), 71), part)
    value_proj = bell_draw(part_splits[4], (TOKENS, HEADS * HD), 1.0, 6.0, ((0, 16), (1, 8)))
    value_tangent = bell_draw(part_splits[5], (TOKENS, HEADS * HD), 1.0, 6.0, ((0, 16), (1, 8)))
    residual = bell_draw(part_splits[6], (TOKENS, D), 1.0, 6.0, ((0, 16), (1, 8)))
    residual_tangent = bell_draw(part_splits[7], (TOKENS, D), 1.0, 6.0, ((0, 16), (1, 8)))
    out_weight = bell_draw_with(key_of[8], (HEADS * HD, D), (HEADS * HD) ** -0.5, 0.15625, ((0, 8),), (0, 1, 8, 2.0))
    out_gate = jnp.clip(0.5 + 1.0 * jax.random.uniform(part_splits[9], (D,), jnp.float32) ** block_levels(part_splits[9], (D,), ((0, 8),), -0.2, 0.2), 0.5, 1.5)
    out_gate_tangent = bell_draw(part_splits[10], (D,), 0.5, 3.0, ((0, 8),), jnp.float32)
    return {"query_proj": query_proj, "query_tangent": query_tangent, "key_proj": key_proj, "key_tangent": key_tangent, "value_proj": value_proj, "value_tangent": value_tangent, "residual": residual, "residual_tangent": residual_tangent, "out_weight": out_weight, "out_gate": out_gate, "out_gate_tangent": out_gate_tangent}


def one_head(arrays):
    queries, query_t, keys, key_t, values, value_t = arrays
    score_scale = HD ** -0.5
    scores = score_scale * jnp.dot(queries, keys.T, preferred_element_type=jnp.float32)
    tangent_scores = score_scale * (jnp.dot(query_t, keys.T, preferred_element_type=jnp.float32)
                                    + jnp.dot(queries, key_t.T, preferred_element_type=jnp.float32))
    weights = jnp.exp(scores - jnp.max(scores, axis=1, keepdims=True))
    total = jnp.sum(weights, axis=1)
    mixed = weights * tangent_scores
    mixed_sum = jnp.sum(mixed, axis=1)
    weights_low = weights.astype(jnp.bfloat16)
    mixed_low = mixed.astype(jnp.bfloat16)
    acc_out = jnp.dot(weights_low, values, preferred_element_type=jnp.float32)
    acc_tan = (jnp.dot(mixed_low, values, preferred_element_type=jnp.float32)
               + jnp.dot(weights_low, value_t, preferred_element_type=jnp.float32))
    attention = (acc_out / total[:, None]).astype(jnp.bfloat16)
    tangent = ((acc_tan - (mixed_sum / total)[:, None] * acc_out) / total[:, None]).astype(jnp.bfloat16)
    return attention, tangent


def by_heads(array):
    return array.reshape(TOKENS, HEADS, HD).transpose(1, 0, 2)


def reference(query_proj, query_tangent, key_proj, key_tangent, value_proj, value_tangent,
              residual, residual_tangent, out_weight, out_gate, out_gate_tangent):
    arrays = tuple(by_heads(item) for item in (query_proj, query_tangent, key_proj, key_tangent,
                                                value_proj, value_tangent))
    attention, tangent = lax.map(one_head, arrays)
    attention = attention.transpose(1, 0, 2).reshape(TOKENS, HEADS * HD)
    tangent = tangent.transpose(1, 0, 2).reshape(TOKENS, HEADS * HD)
    group_width = HEADS * HD // N_HEAD
    projected = jnp.zeros((TOKENS, D), jnp.float32)
    projected_tangent = jnp.zeros((TOKENS, D), jnp.float32)
    for group in range(N_HEAD):
        lower = group * group_width
        rows = out_weight[lower:lower + group_width]
        part_out = jnp.dot(attention[:, lower:lower + group_width], rows,
                           preferred_element_type=jnp.float32).astype(jnp.bfloat16)
        part_tan = jnp.dot(tangent[:, lower:lower + group_width], rows,
                           preferred_element_type=jnp.float32).astype(jnp.bfloat16)
        part_out, part_tan = lax.optimization_barrier((part_out, part_tan))
        projected = projected + part_out.astype(jnp.float32)
        projected_tangent = projected_tangent + part_tan.astype(jnp.float32)
    block_out = (residual.astype(jnp.float32) + out_gate[None, :] * projected).astype(jnp.bfloat16)
    block_tangent = (residual_tangent.astype(jnp.float32) + out_gate_tangent[None, :] * projected
                     + out_gate[None, :] * projected_tangent).astype(jnp.bfloat16)
    return block_out, block_tangent
```

```python
import functools

import jax
import jax.numpy as jnp
from jax import lax
from jax.experimental import pallas as pl
from jax.experimental.pallas import tpu as pltpu
from jax.sharding import Mesh
from jax.sharding import PartitionSpec as P

HD = 128
SCALE = HD ** (-0.5)
SCALE2 = SCALE * 1.4426950408889634
NT = (((1,), (1,)), ((), ()))
BF16 = jnp.bfloat16
F32 = jnp.float32
VMEM_LIMIT = 48 * 1024 * 1024
STATS = 8


def spec_whole():
    return pl.BlockSpec(memory_space=pltpu.VMEM)


def params():
    return pltpu.CompilerParams(vmem_limit_bytes=VMEM_LIMIT)


def pack_kernel(q, qt, k, kt, v, vt, q2, *packs):
    heads = len(packs)
    rows = q.shape[0]
    for h in range(heads):
        cols = slice(h * HD, (h + 1) * HD)
        out = packs[h]
        out[0:rows, 0:HD] = k[:, cols]
        out[0:rows, HD : 2 * HD] = kt[:, cols]
        out[rows : rows + HD, :] = v[:, cols].T
        out[rows + HD : rows + 2 * HD, :] = vt[:, cols].T
        q2[:, 2 * h * HD : (2 * h + 1) * HD] = qt[:, cols]
        q2[:, (2 * h + 1) * HD : (2 * h + 2) * HD] = q[:, cols]


def pack(q, qt, k, kt, v, vt):
    rows, width = q.shape
    heads = width // HD
    return pl.pallas_call(
        pack_kernel,
        out_shape=[jax.ShapeDtypeStruct((rows, 2 * width), BF16)]
        + [jax.ShapeDtypeStruct((rows + 2 * HD, 2 * HD), BF16)] * heads,
        in_specs=[spec_whole()] * 6,
        out_specs=[spec_whole()] * (1 + heads),
        compiler_params=params(),
        cost_estimate=pl.CostEstimate(flops=0, bytes_accessed=24 * rows * width, transcendentals=0),
        name="pack",
    )(q, qt, k, kt, v, vt)


def three_parts(value):
    high = value.astype(BF16)
    rest = value - high.astype(F32)
    middle = rest.astype(BF16)
    low = (rest - middle.astype(F32)).astype(BF16)
    return [high, middle, low]


def attend_kernel(blocks, halves, with_state, final, *refs):
    refs = list(refs)
    q_refs = [refs.pop(0), refs.pop(0)]
    block_refs = [(r, 0, r, 1) for r in [refs.pop(0) for _ in range(blocks)]]
    if halves:
        first, second = refs.pop(0), refs.pop(0)
        block_refs.append((first, 0, second, 0))
    state = refs.pop(0) if with_state else None
    scores_ref = refs.pop()
    rows = q_refs[0].shape[0]
    keys = rows
    for group in range(2):
        q2 = q_refs[group][...]
        q = q2[:, HD:]
        base = group * (2 * HD + STATS)
        top = state[base + 2 * HD : base + 2 * HD + 1, :] if with_state else None
        old_top = top
        for i, (kr, ki, _, _) in enumerate(block_refs):
            part = kr[ki * keys : (ki + 1) * keys, 0:HD]
            scores = lax.dot_general(part, q, NT, preferred_element_type=F32)
            scores_ref[i * keys : (i + 1) * keys, :] = scores
            peak = jnp.max(scores, axis=0, keepdims=True) * SCALE2
            top = peak if top is None else jnp.maximum(top, peak)
        total = jnp.zeros((1, rows), F32)
        mixed_sum = jnp.zeros((1, rows), F32)
        acc = jnp.zeros((2 * HD, rows), F32)
        acc_mixed = jnp.zeros((HD, rows), F32)
        for i, (kr, ki, vr, vi) in enumerate(block_refs):
            kk = kr[ki * keys : (ki + 1) * keys, :]
            tangent = lax.dot_general(kk, q2, NT, preferred_element_type=F32)
            weights = jnp.exp2(scores_ref[i * keys : (i + 1) * keys, :] * SCALE2 - top)
            mixed = weights * tangent
            total = total + jnp.sum(weights, axis=0, keepdims=True)
            mixed_sum = mixed_sum + jnp.sum(mixed, axis=0, keepdims=True)
            vv = vr[vi * keys : vi * keys + 2 * HD, :]
            acc = acc + jnp.dot(vv, weights.astype(BF16), preferred_element_type=F32)
            acc_mixed = acc_mixed + jnp.dot(
                vv[0:HD, :], mixed.astype(BF16), preferred_element_type=F32
            )
        acc_out = acc[0:HD, :]
        acc_tan = acc[HD:, :] + SCALE * acc_mixed
        mixed_sum = SCALE * mixed_sum
        if with_state:
            shrink = jnp.exp2(old_top - top)
            acc_out = acc_out + shrink * state[base : base + HD, :]
            acc_tan = acc_tan + shrink * state[base + HD : base + 2 * HD, :]
            total = total + shrink * state[base + 2 * HD + 1 : base + 2 * HD + 2, :]
            mixed_sum = mixed_sum + shrink * state[base + 2 * HD + 2 : base + 2 * HD + 3, :]
        if not final:
            out = refs[0]
            out[base : base + HD, :] = acc_out
            out[base + HD : base + 2 * HD, :] = acc_tan
            out[base + 2 * HD : base + 2 * HD + 1, :] = top
            out[base + 2 * HD + 1 : base + 2 * HD + 2, :] = total
            out[base + 2 * HD + 2 : base + 2 * HD + 3, :] = mixed_sum
            continue
        inverse = 1.0 / total
        ratio = mixed_sum * inverse
        attention = acc_out * inverse
        attention_t = acc_tan * inverse - ratio * attention
        if group == 0:
            out = refs[0]
            out[0:HD, :] = attention
            out[HD : 2 * HD, :] = attention_t
            out[2 * HD : 2 * HD + 1, :] = top
            out[2 * HD + 1 : 2 * HD + 2, :] = total
            out[2 * HD + 2 : 2 * HD + 3, :] = ratio
        else:
            out = refs[1]
            out[0:HD, :] = attention.astype(BF16)
            out[HD : 2 * HD, :] = attention_t.astype(BF16)
            stats = three_parts(top) + three_parts(total) + three_parts(ratio)
            stats = [s.astype(F32) for s in stats]
            stats.append(jnp.zeros((2 * STATS - len(stats), rows), F32))
            out[2 * HD :, :] = jnp.concatenate(stats, axis=0).astype(BF16)


def attend(head, q_own, q_far, blocks, halves=(), state=None, final=False):
    rows = q_own.shape[0]
    n = len(blocks) + (1 if halves else 0)
    q_spec = pl.BlockSpec((rows, 2 * HD), lambda i: (0, head))
    tall = 2 * HD + STATS
    whole = lambda a: pl.BlockSpec(a.shape, lambda i: (0, 0))
    extra = list(blocks) + list(halves) + ([state] if state is not None else [])
    if final:
        outs = [
            jax.ShapeDtypeStruct((tall, rows), F32),
            jax.ShapeDtypeStruct((2 * HD + 2 * STATS, rows), BF16),
        ]
    else:
        outs = [jax.ShapeDtypeStruct((2 * tall, rows), F32)]
    result = pl.pallas_call(
        functools.partial(attend_kernel, len(blocks), bool(halves), state is not None, final),
        grid=(1,),
        out_shape=outs,
        in_specs=[q_spec, q_spec] + [whole(a) for a in extra],
        out_specs=[whole(a) for a in outs],
        scratch_shapes=[pltpu.VMEM((n * rows, rows), F32)],
        compiler_params=params(),
        cost_estimate=pl.CostEstimate(
            flops=2 * 2 * rows * n * rows * HD * 8,
            bytes_accessed=2 * rows * HD * 4 * (n + 2),
            transcendentals=2 * rows * n * rows,
        ),
        name="attend",
    )(q_own, q_far, *extra)
    return result if final else result[0]


def merge_kernel(own, far, out):
    rows = own.shape[1]
    stats = far[2 * HD :, :].astype(F32)
    pick = lambda i: stats[3 * i : 3 * i + 1] + stats[3 * i + 1 : 3 * i + 2] + stats[3 * i + 2 : 3 * i + 3]
    top0, total0, ratio0 = (own[2 * HD + i : 2 * HD + i + 1, :] for i in range(3))
    top1, total1, ratio1 = pick(0), pick(1), pick(2)
    top = jnp.maximum(top0, top1)
    part0 = total0 * jnp.exp2(top0 - top)
    part1 = total1 * jnp.exp2(top1 - top)
    inverse = 1.0 / (part0 + part1)
    part0, part1 = part0 * inverse, part1 * inverse
    att0, att1 = own[0:HD, :], far[0:HD, :].astype(F32)
    tan0, tan1 = own[HD : 2 * HD, :], far[HD : 2 * HD, :].astype(F32)
    attention = part0 * att0 + part1 * att1
    tangent = part0 * tan0 + part1 * tan1 + (part0 * part1 * (ratio0 - ratio1)) * (att0 - att1)
    out[0:rows, :] = attention.T.astype(BF16)
    out[rows:, :] = tangent.T.astype(BF16)


def merge(own, far):
    rows = own.shape[1]
    return pl.pallas_call(
        merge_kernel,
        out_shape=jax.ShapeDtypeStruct((2 * rows, HD), BF16),
        in_specs=[spec_whole()] * 2,
        out_specs=spec_whole(),
        compiler_params=params(),
        cost_estimate=pl.CostEstimate(flops=0, bytes_accessed=rows * HD * 14, transcendentals=0),
        name="merge",
    )(own, far)


def project_kernel(heads, count, with_acc, *refs):
    refs = list(refs)
    atts = [[refs.pop(0) for _ in range(count)] for _ in heads]
    weights = [refs.pop(0) for _ in range(count)]
    acc = refs.pop(0) if with_acc else None
    out = refs.pop(0)
    total = None
    for place, head in enumerate(heads):
        for d in range(0, count, 2):
            left = jnp.concatenate([atts[place][d][...], atts[place][d + 1][...]], axis=1)
            rows = slice(head * HD, (head + 1) * HD)
            right = jnp.concatenate([weights[d][rows, :], weights[d + 1][rows, :]], axis=0)
            term = jnp.dot(left, right, preferred_element_type=F32)
            total = term if total is None else total + term
    if with_acc:
        total = total + acc[...]
    out[...] = total.astype(out.dtype)


def project(heads, atts, weights, half, acc, dtype):
    count = len(weights)
    rows = atts[0][0].shape[0]
    depth, width = weights[0].shape
    cols = width // 2
    step = 256
    whole = pl.BlockSpec((rows, HD), lambda i: (0, 0))
    first = half * (cols // step)
    w_spec = pl.BlockSpec((depth, step), lambda i: (0, first + i))
    acc_spec = pl.BlockSpec((rows, step), lambda i: (0, i))
    flat = [a for group in atts for a in group]
    extra = [] if acc is None else [acc]
    return pl.pallas_call(
        functools.partial(project_kernel, heads, count, acc is not None),
        grid=(cols // step,),
        out_shape=jax.ShapeDtypeStruct((rows, cols), dtype),
        in_specs=[whole] * len(flat) + [w_spec] * count + [acc_spec] * len(extra),
        out_specs=acc_spec,
        compiler_params=params(),
        cost_estimate=pl.CostEstimate(
            flops=2 * rows * cols * HD * count * len(heads),
            bytes_accessed=rows * cols * 6 + depth * cols * 2 * count,
            transcendentals=0,
        ),
        name="project",
    )(*flat, *weights, *extra)


def ring_pairs(size, shift):
    return [(i, (i + shift) % size) for i in range(size)]


def per_device(sizes, q, qt, k, kt, v, vt, residual, residual_t, weight, gate, gate_t):
    n_z, n_x = sizes
    rows = q.shape[0]
    heads = q.shape[1] // HD
    features = residual.shape[1]
    q_own, *packs = pack(q, qt, k, kt, v, vt)
    swap = [(0, 1), (1, 0)]
    q_far = lax.ppermute(q_own, "y_hi", swap)
    up, down = ring_pairs(n_z, 1), ring_pairs(n_z, -1)

    arrivals = []
    for h in range(heads):
        start = packs[h]
        if h > 0:
            start, _ = lax.optimization_barrier((start, arrivals[h - 1][1]))
        forward, backward = start, start
        steps = []
        for _ in range((n_z - 1) // 2):
            forward = lax.ppermute(forward, "z", up)
            backward = lax.ppermute(backward, "z", down)
            steps.append((forward, backward))
        last_k = lax.ppermute(forward[0:rows], "z", up)
        last_v = lax.ppermute(backward[rows:], "z", down)
        steps.append((last_k, last_v))
        arrivals.append(steps)

    core = lax.axis_index("core")
    place = lax.axis_index("x")
    blocks = []
    for d in range(n_x):
        target = lax.rem(place + d, n_x)
        mine = lax.dynamic_slice_in_dim(weight, (2 * target + core) * features, features, 1)
        other = lax.dynamic_slice_in_dim(weight, (2 * target + 1 - core) * features, features, 1)
        block = jnp.concatenate([mine, other], axis=1)
        blocks.append(block if d == 0 else lax.ppermute(block, "x", ring_pairs(n_x, d)))

    gathered = []
    for h in range(heads):
        steps = arrivals[h]
        early = [packs[h]] + [b for s in steps[:2] for b in s]
        late = [b for s in steps[2:-1] for b in s]
        state = attend(h, q_own, q_far, early)
        own, to_far = attend(h, q_own, q_far, late, halves=steps[-1], state=state, final=True)
        from_far = lax.ppermute(to_far, "y_hi", swap)
        att = merge(own, from_far)
        gathered.append(
            [att] + [lax.ppermute(att, "x", ring_pairs(n_x, d)) for d in range(1, n_x)]
        )
    before, last = tuple(range(heads - 1)), (heads - 1,)
    acc_other = project(before, gathered[:-1], blocks, 1, None, F32)
    acc_own = project(before, gathered[:-1], blocks, 0, None, F32)
    to_core = project(last, gathered[-1:], blocks, 1, acc_other, BF16)
    from_core = lax.ppermute(to_core, "core", swap)
    mine = project(last, gathered[-1:], blocks, 0, acc_own, F32)
    summed = mine + from_core.astype(F32)
    projected, projected_t = summed[:rows], summed[rows:]
    block_out = (residual.astype(F32) + gate[None, :] * projected).astype(BF16)
    block_tangent = (
        residual_t.astype(F32) + gate_t[None, :] * projected + gate[None, :] * projected_t
    ).astype(BF16)
    return block_out, block_tangent


def solution(mesh):
    n_z, n_x = mesh.shape["seq"] // 2, mesh.shape["head"] // 2
    fine = Mesh(
        mesh.devices.reshape(n_z, 2, n_x, 2, mesh.shape["dp"]), ("z", "y_hi", "x", "core", "dp")
    )
    tokens, width = ("dp", "z", "y_hi"), ("x", "core")
    wide = P(tokens, width)
    gates = P(("dp", "x", "core"))
    return jax.shard_map(
        functools.partial(per_device, (n_z, n_x)),
        mesh=fine,
        in_specs=(wide,) * 8 + (P(width, None), gates, gates),
        out_specs=(wide, wide),
        check_vma=False,
    )
```

```python
import functools

import jax
import jax.numpy as jnp
from jax import lax
from jax.experimental import pallas as pl
from jax.experimental.pallas import tpu as pltpu
from jax.sharding import Mesh
from jax.sharding import PartitionSpec as P

HD = 128
SCALE = HD ** (-0.5)
SCALE2 = SCALE * 1.4426950408889634
NT = (((1,), (1,)), ((), ()))
BF16 = jnp.bfloat16
F32 = jnp.float32
VMEM_LIMIT = 48 * 1024 * 1024
STATS = 8


def spec_whole():
    return pl.BlockSpec(memory_space=pltpu.VMEM)


def params():
    return pltpu.CompilerParams(vmem_limit_bytes=VMEM_LIMIT)


def query_kernel(q, qt, out):
    out[:, 0:HD] = qt[...]
    out[:, HD:] = q[...]


def pack_queries(q, qt):
    rows, width = q.shape
    spec = pl.BlockSpec((rows, HD), lambda h: (0, h))
    return pl.pallas_call(
        query_kernel,
        grid=(width // HD,),
        out_shape=jax.ShapeDtypeStruct((rows, 2 * width), BF16),
        in_specs=[spec] * 2,
        out_specs=pl.BlockSpec((rows, 2 * HD), lambda h: (0, h)),
        compiler_params=params(),
        cost_estimate=pl.CostEstimate(flops=0, bytes_accessed=8 * rows * width, transcendentals=0),
        name="pack_queries",
    )(q, qt)


def pack_kernel(k, kt, v, vt, out):
    out[0, :, 0:HD] = k[...]
    out[0, :, HD:] = kt[...]
    out[1, 0:HD, :] = v[...].T
    out[1, HD:, :] = vt[...].T


def pack(k, kt, v, vt, first, heads):
    rows = k.shape[0]
    spec = pl.BlockSpec((rows, HD), lambda h: (0, first + h))
    out = pl.pallas_call(
        pack_kernel,
        grid=(heads,),
        out_shape=jax.ShapeDtypeStruct((2, heads * 2 * HD, rows), BF16),
        in_specs=[spec] * 4,
        out_specs=pl.BlockSpec((2, 2 * HD, rows), lambda h: (0, h, 0)),
        compiler_params=params(),
        cost_estimate=pl.CostEstimate(
            flops=0, bytes_accessed=16 * rows * heads * HD, transcendentals=0
        ),
        name="pack",
    )(k, kt, v, vt)
    return out


def three_parts(value):
    high = value.astype(BF16)
    rest = value - high.astype(F32)
    middle = rest.astype(BF16)
    low = (rest - middle.astype(F32)).astype(BF16)
    return [high, middle, low]


def attend_kernel(blocks, with_state, final, *refs):
    refs = list(refs)
    q_refs = [refs.pop(0), refs.pop(0)]
    k_refs = [refs.pop(0) for _ in range(blocks)]
    v_refs = [refs.pop(0) for _ in range(blocks)]
    state = refs.pop(0) if with_state else None
    scores_ref = refs.pop()
    rows = q_refs[0].shape[0]
    keys = rows
    for group in range(2):
        q2 = q_refs[group][...]
        q = q2[:, HD:]
        base = group * (2 * HD + STATS)
        top = state[base + 2 * HD : base + 2 * HD + 1, :] if with_state else None
        old_top = top
        for i, k_ref in enumerate(k_refs):
            part = k_ref[:, 0:HD]
            scores = lax.dot_general(part, q, NT, preferred_element_type=F32)
            scores_ref[i * keys : (i + 1) * keys, :] = scores
            peak = jnp.max(scores, axis=0, keepdims=True) * SCALE2
            top = peak if top is None else jnp.maximum(top, peak)
        total = jnp.zeros((1, rows), F32)
        mixed_sum = jnp.zeros((1, rows), F32)
        acc = jnp.zeros((2 * HD, rows), F32)
        acc_mixed = jnp.zeros((HD, rows), F32)
        for i, (k_ref, v_ref) in enumerate(zip(k_refs, v_refs)):
            tangent = lax.dot_general(k_ref[...], q2, NT, preferred_element_type=F32)
            weights = jnp.exp2(scores_ref[i * keys : (i + 1) * keys, :] * SCALE2 - top)
            mixed = weights * tangent
            total = total + jnp.sum(weights, axis=0, keepdims=True)
            mixed_sum = mixed_sum + jnp.sum(mixed, axis=0, keepdims=True)
            vv = v_ref[...]
            acc = acc + jnp.dot(vv, weights.astype(BF16), preferred_element_type=F32)
            acc_mixed = acc_mixed + jnp.dot(
                vv[0:HD, :], mixed.astype(BF16), preferred_element_type=F32
            )
        acc_out = acc[0:HD, :]
        acc_tan = acc[HD:, :] + SCALE * acc_mixed
        mixed_sum = SCALE * mixed_sum
        if with_state:
            shrink = jnp.exp2(old_top - top)
            acc_out = acc_out + shrink * state[base : base + HD, :]
            acc_tan = acc_tan + shrink * state[base + HD : base + 2 * HD, :]
            total = total + shrink * state[base + 2 * HD + 1 : base + 2 * HD + 2, :]
            mixed_sum = mixed_sum + shrink * state[base + 2 * HD + 2 : base + 2 * HD + 3, :]
        if not final:
            out = refs[0]
            out[base : base + HD, :] = acc_out
            out[base + HD : base + 2 * HD, :] = acc_tan
            out[base + 2 * HD : base + 2 * HD + 1, :] = top
            out[base + 2 * HD + 1 : base + 2 * HD + 2, :] = total
            out[base + 2 * HD + 2 : base + 2 * HD + 3, :] = mixed_sum
            continue
        inverse = 1.0 / total
        ratio = mixed_sum * inverse
        attention = acc_out * inverse
        attention_t = acc_tan * inverse - ratio * attention
        if group == 0:
            out = refs[0]
            out[0:HD, :] = attention
            out[HD : 2 * HD, :] = attention_t
            out[2 * HD : 2 * HD + 1, :] = top
            out[2 * HD + 1 : 2 * HD + 2, :] = total
            out[2 * HD + 2 : 2 * HD + 3, :] = ratio
        else:
            out = refs[1]
            out[0:HD, :] = attention.astype(BF16)
            out[HD : 2 * HD, :] = attention_t.astype(BF16)
            stats = three_parts(top) + three_parts(total) + three_parts(ratio)
            stats = [s.astype(F32) for s in stats]
            stats.append(jnp.zeros((2 * STATS - len(stats), rows), F32))
            out[2 * HD :, :] = jnp.concatenate(stats, axis=0).astype(BF16)


def attend(first, heads, q_own, q_far, blocks, state=None, final=False):
    rows = q_own.shape[0]
    n = len(blocks)
    q_spec = pl.BlockSpec((rows, 2 * HD), lambda h: (0, first + h))
    tall, far = 2 * HD + STATS, 2 * HD + 2 * STATS
    keys, values, specs = [], [], []
    for block in blocks:
        pair = block if isinstance(block, tuple) else (block, block)
        keys.append(pair[0])
        values.append(pair[1])
    for group, part in ((keys, 0), (values, 1)):
        for array in group:
            if array.ndim == 3:
                specs.append(pl.BlockSpec((None, 2 * HD, rows), lambda h, p=part: (p, h, 0)))
            else:
                specs.append(pl.BlockSpec((2 * HD, rows), lambda h: (h, 0)))
    by_head = lambda height: pl.BlockSpec((height, rows), lambda h: (h, 0))
    extra = []
    if state is not None:
        extra.append(state)
        specs.append(by_head(2 * tall))
    if final:
        outs = [
            jax.ShapeDtypeStruct((heads * tall, rows), F32),
            jax.ShapeDtypeStruct((heads * far, rows), BF16),
        ]
        out_specs = [by_head(tall), by_head(far)]
    else:
        outs = [jax.ShapeDtypeStruct((heads * 2 * tall, rows), F32)]
        out_specs = [by_head(2 * tall)]
    result = pl.pallas_call(
        functools.partial(attend_kernel, n, state is not None, final),
        grid=(heads,),
        out_shape=outs,
        in_specs=[q_spec, q_spec] + specs,
        out_specs=out_specs,
        scratch_shapes=[pltpu.VMEM((n * rows, rows), F32)],
        compiler_params=params(),
        cost_estimate=pl.CostEstimate(
            flops=heads * 2 * 2 * rows * n * rows * HD * 8,
            bytes_accessed=heads * 2 * rows * HD * 4 * (n + 2),
            transcendentals=heads * 2 * rows * n * rows,
        ),
        name="attend",
    )(q_own, q_far, *keys, *values, *extra)
    return result if final else result[0]


def merge_kernel(own, far, out):
    rows = own.shape[1]
    stats = far[2 * HD :, :].astype(F32)
    pick = lambda i: stats[3 * i : 3 * i + 1] + stats[3 * i + 1 : 3 * i + 2] + stats[3 * i + 2 : 3 * i + 3]
    top0, total0, ratio0 = (own[2 * HD + i : 2 * HD + i + 1, :] for i in range(3))
    top1, total1, ratio1 = pick(0), pick(1), pick(2)
    top = jnp.maximum(top0, top1)
    part0 = total0 * jnp.exp2(top0 - top)
    part1 = total1 * jnp.exp2(top1 - top)
    inverse = 1.0 / (part0 + part1)
    part0, part1 = part0 * inverse, part1 * inverse
    att0, att1 = own[0:HD, :], far[0:HD, :].astype(F32)
    tan0, tan1 = own[HD : 2 * HD, :], far[HD : 2 * HD, :].astype(F32)
    attention = part0 * att0 + part1 * att1
    tangent = part0 * tan0 + part1 * tan1 + (part0 * part1 * (ratio0 - ratio1)) * (att0 - att1)
    out[0:rows, :] = attention.T.astype(BF16)
    out[rows:, :] = tangent.T.astype(BF16)


def merge(heads, own, far):
    rows = own.shape[1]
    tall, far_tall = own.shape[0] // heads, far.shape[0] // heads
    return pl.pallas_call(
        merge_kernel,
        grid=(heads,),
        out_shape=jax.ShapeDtypeStruct((2 * rows, heads * HD), BF16),
        in_specs=[
            pl.BlockSpec((tall, rows), lambda h: (h, 0)),
            pl.BlockSpec((far_tall, rows), lambda h: (h, 0)),
        ],
        out_specs=pl.BlockSpec((2 * rows, HD), lambda h: (0, h)),
        compiler_params=params(),
        cost_estimate=pl.CostEstimate(
            flops=0, bytes_accessed=heads * rows * HD * 14, transcendentals=0
        ),
        name="merge",
    )(own, far)


def project_kernel(first, heads, with_acc, *refs):
    refs = list(refs)
    out = refs.pop()
    acc = refs.pop() if with_acc else None
    shared, local = refs.pop(), refs.pop()
    left = jnp.concatenate([r[...] for r in refs], axis=1)
    rows = slice(first * HD, (first + heads) * HD)
    right = [local[rows, :]] + [shared[d, rows, :] for d in range(shared.shape[0])]
    total = jnp.dot(left, jnp.concatenate(right, axis=0), preferred_element_type=F32)
    if with_acc:
        total = total + acc[...]
    out[...] = total.astype(out.dtype)


def project(first, heads, atts, local, shared, half, acc, dtype):
    rows = atts[0].shape[0]
    quarters, others, depth, step = shared.shape
    count = quarters // 2
    whole = pl.BlockSpec((rows, heads * HD), lambda i: (0, 0))
    acc_spec = pl.BlockSpec((rows, step), lambda i: (0, i))
    extra = [] if acc is None else [acc]
    return pl.pallas_call(
        functools.partial(project_kernel, first, heads, acc is not None),
        grid=(count,),
        out_shape=jax.ShapeDtypeStruct((rows, count * step), dtype),
        in_specs=[whole] * len(atts)
        + [
            pl.BlockSpec((depth, step), lambda i: (0, half * count + i)),
            pl.BlockSpec((None, others, depth, step), lambda i: (half * count + i, 0, 0, 0)),
        ]
        + [acc_spec] * len(extra),
        out_specs=acc_spec,
        compiler_params=params(),
        cost_estimate=pl.CostEstimate(
            flops=2 * rows * count * step * HD * len(atts) * heads,
            bytes_accessed=rows * count * step * 6 + depth * count * step * 8,
            transcendentals=0,
        ),
        name="project",
    )(*atts, local, shared, *extra)


def finish_kernel(mine, other, res, res_t, gate, gate_t, out, out_t):
    rows = res.shape[0]
    projected = mine[0:rows, :] + other[0:rows, :].astype(F32)
    projected_t = mine[rows:, :] + other[rows:, :].astype(F32)
    g = gate[...]
    out[...] = (res[...].astype(F32) + g * projected).astype(out.dtype)
    out_t[...] = (res_t[...].astype(F32) + gate_t[...] * projected + g * projected_t).astype(
        out_t.dtype
    )


def finish(mine, other, res, res_t, gate, gate_t):
    rows, width = res.shape
    step = 256
    tall = pl.BlockSpec((2 * rows, step), lambda i: (0, i))
    short = pl.BlockSpec((rows, step), lambda i: (0, i))
    line = pl.BlockSpec((1, step), lambda i: (0, i))
    return pl.pallas_call(
        finish_kernel,
        grid=(width // step,),
        out_shape=[jax.ShapeDtypeStruct((rows, width), BF16)] * 2,
        in_specs=[tall, tall, short, short, line, line],
        out_specs=[short, short],
        compiler_params=params(),
        cost_estimate=pl.CostEstimate(flops=0, bytes_accessed=rows * width * 20, transcendentals=0),
        name="finish",
    )(mine, other, res, res_t, gate[None, :], gate_t[None, :])


def ring_pairs(size, shift):
    return [(i, (i + shift) % size) for i in range(size)]


def after(value, *others):
    return lax.optimization_barrier((value,) + others)[0]


def per_device(sizes, q, qt, k, kt, v, vt, residual, residual_t, weight, gate, gate_t):
    n_z, n_x = sizes
    heads = q.shape[1] // HD
    features = residual.shape[1]
    groups = [(0, heads - 1), (heads - 1, 1)]
    swap = [(0, 1), (1, 0)]
    up, down = ring_pairs(n_z, 1), ring_pairs(n_z, -1)
    packs = [pack(k, kt, v, vt, first, count) for first, count in groups]
    q_own = pack_queries(q, qt)
    q_far = lax.ppermute(q_own, "y_hi", swap)

    arrivals = []
    for place, start in enumerate(packs):
        if place > 0:
            start = after(start, arrivals[0][0][0])
        forward, backward = start, start
        steps = []
        for _ in range((n_z - 1) // 2):
            forward = lax.ppermute(forward, "z", up)
            backward = lax.ppermute(backward, "z", down)
            steps.append((forward, backward))
        last_k = lax.ppermute(forward[0], "z", up)
        last_v = lax.ppermute(backward[1], "z", down)
        steps.append((last_k, last_v))
        arrivals.append(steps)

    core = lax.axis_index("core")
    place = lax.axis_index("x")
    shares = 4
    share = 2 * lax.axis_index("y_hi") + lax.axis_index("dp")
    step = 2 * features // shares
    half = share // (shares // 2)
    inner = lax.rem(share, shares // 2) * step
    pieces = []
    for d in range(1, n_x):
        target = lax.rem(place + d, n_x)
        column = (2 * target + lax.rem(core + half, 2)) * features + inner
        piece = lax.dynamic_slice_in_dim(weight, column, step, 1)
        pieces.append(lax.ppermute(piece, "x", ring_pairs(n_x, d)))
    shared = lax.all_gather(jnp.stack(pieces), ("y_hi", "dp"), axis=0)
    local = jnp.concatenate(
        [
            lax.dynamic_slice_in_dim(weight, (2 * place + core) * features, features, 1),
            lax.dynamic_slice_in_dim(weight, (2 * place + 1 - core) * features, features, 1),
        ],
        axis=1,
    )

    gathered = []
    for (first, count), own_pack, steps in zip(groups, packs, arrivals):
        run = functools.partial(attend, first, count, q_own, q_far)
        state = run([own_pack] + [b for s in steps[:2] for b in s])
        late = list(steps[2]) + [steps[3]]
        if first > 0:
            state = run(late[:-1], state=state)
            late = late[-1:]
        own, to_far = run(late, state=state, final=True)
        att = merge(count, own, lax.ppermute(to_far, "y_hi", swap))
        gathered.append(
            [att] + [lax.ppermute(att, "x", ring_pairs(n_x, d)) for d in range(1, n_x)]
        )
    run = functools.partial(project, *groups[0], gathered[0], local, shared)
    acc_other, acc_own = run(1, None, F32), run(0, None, F32)
    run = functools.partial(project, *groups[1], gathered[1], local, shared)
    to_core = run(1, acc_other, BF16)
    from_core = lax.ppermute(to_core, "core", swap)
    mine = run(0, acc_own, F32)
    return tuple(finish(mine, from_core, residual, residual_t, gate, gate_t))


def solution(mesh):
    n_z, n_x = mesh.shape["seq"] // 2, mesh.shape["head"] // 2
    fine = Mesh(
        mesh.devices.reshape(n_z, 2, n_x, 2, mesh.shape["dp"]), ("z", "y_hi", "x", "core", "dp")
    )
    tokens, width = ("dp", "z", "y_hi"), ("x", "core")
    wide = P(tokens, width)
    gates = P(("dp", "x", "core"))
    return jax.shard_map(
        functools.partial(per_device, (n_z, n_x)),
        mesh=fine,
        in_specs=(wide,) * 8 + (P(width, None), gates, gates),
        out_specs=(wide, wide),
        check_vma=False,
    )
```

```python
import functools

import jax
import jax.numpy as jnp
from jax import lax
from jax.experimental import pallas as pl
from jax.experimental.pallas import tpu as pltpu
from jax.sharding import Mesh
from jax.sharding import PartitionSpec as P

HD = 128
SCALE = HD ** (-0.5)
SCALE2 = SCALE * 1.4426950408889634
NT = (((1,), (1,)), ((), ()))
BF16 = jnp.bfloat16
F32 = jnp.float32
STATS = 8


def spec_whole():
    return pl.BlockSpec(memory_space=pltpu.VMEM)


def params(mib=12):
    return pltpu.CompilerParams(vmem_limit_bytes=mib * 1024 * 1024)


def query_kernel(q, qt, out, sems):
    copies = []
    for h in range(q.shape[1] // HD):
        for i, ref in enumerate((qt, q)):
            copies.append(
                pltpu.make_async_copy(
                    ref.at[:, h * HD : (h + 1) * HD],
                    out.at[:, (2 * h + i) * HD : (2 * h + i + 1) * HD],
                    sems.at[2 * h + i],
                )
            )
    for copy in copies:
        copy.start()
    for copy in copies:
        copy.wait()


def pack_queries(q, qt):
    rows, width = q.shape
    return pl.pallas_call(
        query_kernel,
        out_shape=jax.ShapeDtypeStruct((rows, 2 * width), BF16),
        in_specs=[pl.BlockSpec(memory_space=pltpu.HBM)] * 2,
        out_specs=spec_whole(),
        scratch_shapes=[pltpu.SemaphoreType.DMA((2 * width // HD,))],
        compiler_params=params(),
        cost_estimate=pl.CostEstimate(flops=0, bytes_accessed=8 * rows * width, transcendentals=0),
        name="pack_queries",
    )(q, qt)


def pack_kernel(k, kt, v, vt, out, scratch, sems):
    heads = k.shape[1] // HD
    values = [
        pltpu.make_async_copy(ref, scratch.at[i], sems.at[2 * heads + i])
        for i, ref in enumerate((v, vt))
    ]
    copies = []
    for h in range(heads):
        for i, ref in enumerate((k, kt)):
            copies.append(
                pltpu.make_async_copy(
                    ref.at[:, h * HD : (h + 1) * HD],
                    out.at[0, 2 * h * HD : 2 * (h + 1) * HD, i * HD : (i + 1) * HD],
                    sems.at[2 * h + i],
                )
            )
    for copy in values + copies:
        copy.start()
    for i, copy in enumerate(values):
        copy.wait()
        for h in range(heads):
            part = scratch[i, :, h * HD : (h + 1) * HD].T
            out[1, (2 * h + i) * HD : (2 * h + i + 1) * HD, :] = part
    for copy in copies:
        copy.wait()


def pack(k, kt, v, vt):
    rows, width = k.shape
    return pl.pallas_call(
        pack_kernel,
        out_shape=jax.ShapeDtypeStruct((2, 2 * width, rows), BF16),
        in_specs=[pl.BlockSpec(memory_space=pltpu.HBM)] * 4,
        out_specs=spec_whole(),
        scratch_shapes=[
            pltpu.VMEM((2, rows, width), BF16),
            pltpu.SemaphoreType.DMA((2 * width // HD + 2,)),
        ],
        compiler_params=params(),
        cost_estimate=pl.CostEstimate(flops=0, bytes_accessed=16 * rows * width, transcendentals=0),
        name="pack",
    )(k, kt, v, vt)


def three_parts(value):
    high = value.astype(BF16)
    rest = value - high.astype(F32)
    middle = rest.astype(BF16)
    low = (rest - middle.astype(F32)).astype(BF16)
    return [high, middle, low]


def attend_kernel(kinds, groups, with_state, final, *refs):
    refs = list(refs)
    scores_ref = refs.pop()
    q_refs = [refs.pop(0), refs.pop(0)]
    pairs = []
    for halves in kinds:
        if halves:
            pairs.append((refs.pop(0), refs.pop(0)))
        else:
            both = refs.pop(0)
            pairs.append((both.at[0], both.at[1]))
    state = refs.pop(0) if with_state else None
    keys = q_refs[0].shape[0]
    tall, far_tall = 2 * HD + STATS, 2 * HD + 2 * STATS
    where = [(g, i) for g, (_, count) in enumerate(groups) for i in range(count)]
    for h, (group, inner) in enumerate(where):
        place = pl.ds(2 * h * HD, 2 * HD)
        q2 = jnp.concatenate([r[:, place] for r in q_refs], axis=0)
        old = state.at[pl.ds(h * tall, tall), :] if with_state else None
        sums = attend_blocks(
            q2, [(k.at[place, :], v.at[place, :]) for k, v in pairs], old, scores_ref
        )
        acc_out, acc_tan, top, total, mixed_sum = sums
        if not final:
            put(refs[0], h * tall, *sums)
            continue
        inverse = 1.0 / total
        ratio = mixed_sum * inverse
        attention = acc_out * inverse
        attention_t = acc_tan * inverse - ratio * attention
        parts = (attention, attention_t, top, total, ratio)
        own, far = refs[0], refs[1 + group]
        put(own, h * tall, *(p[:, :keys] for p in parts))
        base = inner * far_tall
        far[base : base + HD, :] = attention[:, keys:].astype(BF16)
        far[base + HD : base + 2 * HD, :] = attention_t[:, keys:].astype(BF16)
        stats = three_parts(top) + three_parts(total) + three_parts(ratio)
        stats = [s[:, keys:].astype(F32) for s in stats]
        stats.append(jnp.zeros((2 * STATS - len(stats), keys), F32))
        far[base + 2 * HD : base + far_tall, :] = jnp.concatenate(stats, axis=0).astype(BF16)


def put(out, base, upper, lower, *lines):
    out[base : base + HD, :] = upper
    out[base + HD : base + 2 * HD, :] = lower
    for i, line in enumerate(lines):
        out[base + 2 * HD + i : base + 2 * HD + i + 1, :] = line


def attend_blocks(q2, pairs, state, scores_ref):
    rows = q2.shape[0]
    keys = rows // 2
    q = q2[:, HD:]
    top = state[2 * HD : 2 * HD + 1, :] if state is not None else None
    old_top = top
    for i, (k_ref, _) in enumerate(pairs):
        scores = lax.dot_general(k_ref[:, 0:HD], q, NT, preferred_element_type=F32)
        scores_ref[i * keys : (i + 1) * keys, :] = scores
        peak = jnp.max(scores, axis=0, keepdims=True) * SCALE2
        top = peak if top is None else jnp.maximum(top, peak)
    total = jnp.zeros((1, rows), F32)
    mixed_sum = jnp.zeros((1, rows), F32)
    all_weights, all_mixed = [], []
    for i, (k_ref, _) in enumerate(pairs):
        tangent = lax.dot_general(k_ref[...], q2, NT, preferred_element_type=F32)
        weights = jnp.exp2(scores_ref[i * keys : (i + 1) * keys, :] * SCALE2 - top)
        mixed = weights * tangent
        total = total + jnp.sum(weights, axis=0, keepdims=True)
        mixed_sum = mixed_sum + jnp.sum(mixed, axis=0, keepdims=True)
        all_weights.append(weights.astype(BF16))
        all_mixed.append(mixed.astype(BF16))
    values = jnp.concatenate([v_ref[...] for _, v_ref in pairs], axis=1)
    acc = jnp.dot(values, jnp.concatenate(all_weights, axis=0), preferred_element_type=F32)
    acc_mixed = jnp.dot(
        values[0:HD, :], jnp.concatenate(all_mixed, axis=0), preferred_element_type=F32
    )
    acc_out = acc[0:HD, :]
    acc_tan = acc[HD:, :] + SCALE * acc_mixed
    mixed_sum = SCALE * mixed_sum
    if state is not None:
        shrink = jnp.exp2(old_top - top)
        acc_out = acc_out + shrink * state[0:HD, :]
        acc_tan = acc_tan + shrink * state[HD : 2 * HD, :]
        total = total + shrink * state[2 * HD + 1 : 2 * HD + 2, :]
        mixed_sum = mixed_sum + shrink * state[2 * HD + 2 : 2 * HD + 3, :]
    return acc_out, acc_tan, top, total, mixed_sum


def attend(q_own, q_far, groups, blocks, state=None, final=False):
    rows = q_own.shape[0]
    heads = sum(count for _, count in groups)
    n = len(blocks)
    tall, far = 2 * HD + STATS, 2 * HD + 2 * STATS
    kinds = [isinstance(block, tuple) for block in blocks]
    arrays = [q_own, q_far]
    for block in blocks:
        arrays.extend(block if isinstance(block, tuple) else (block,))
    if state is not None:
        arrays.append(state)
    if final:
        outs = [
            jax.ShapeDtypeStruct((heads * tall, rows), F32),
            *(jax.ShapeDtypeStruct((count * far, rows), BF16) for _, count in groups),
        ]
    else:
        outs = [jax.ShapeDtypeStruct((heads * tall, 2 * rows), F32)]
    result = pl.pallas_call(
        functools.partial(attend_kernel, kinds, groups, state is not None, final),
        out_shape=outs,
        in_specs=[spec_whole()] * len(arrays),
        out_specs=[spec_whole()] * len(outs),
        scratch_shapes=[pltpu.VMEM((n * rows, 2 * rows), F32)],
        compiler_params=params(20),
        cost_estimate=pl.CostEstimate(
            flops=4 * heads * 2 * 2 * rows * n * rows * HD * 8,
            bytes_accessed=heads * 2 * rows * HD * 4 * (n + 2),
            transcendentals=heads * 2 * rows * n * rows,
        ),
        name="attend",
    )(*arrays)
    return result if final else result[0]


def merge_kernel(first, own_ref, far_ref, out):
    rows = own_ref.shape[1]
    tall, far_tall = 2 * HD + STATS, 2 * HD + 2 * STATS
    for h in range(far_ref.shape[0] // far_tall):
        own = own_ref[(first + h) * tall : (first + h + 1) * tall, :]
        far = far_ref[h * far_tall : (h + 1) * far_tall, :]
        attention, tangent = merge_parts(own, far)
        out[0:rows, h * HD : (h + 1) * HD] = attention.T.astype(BF16)
        out[rows:, h * HD : (h + 1) * HD] = tangent.T.astype(BF16)


def merge_parts(own, far):
    stats = far[2 * HD :, :].astype(F32)
    pick = lambda i: stats[3 * i : 3 * i + 1] + stats[3 * i + 1 : 3 * i + 2] + stats[3 * i + 2 : 3 * i + 3]
    top0, total0, ratio0 = (own[2 * HD + i : 2 * HD + i + 1, :] for i in range(3))
    top1, total1, ratio1 = pick(0), pick(1), pick(2)
    top = jnp.maximum(top0, top1)
    part0 = total0 * jnp.exp2(top0 - top)
    part1 = total1 * jnp.exp2(top1 - top)
    inverse = 1.0 / (part0 + part1)
    part0, part1 = part0 * inverse, part1 * inverse
    att0, att1 = own[0:HD, :], far[0:HD, :].astype(F32)
    tan0, tan1 = own[HD : 2 * HD, :], far[HD : 2 * HD, :].astype(F32)
    attention = part0 * att0 + part1 * att1
    tangent = part0 * tan0 + part1 * tan1 + (part0 * part1 * (ratio0 - ratio1)) * (att0 - att1)
    return attention, tangent


def merge(first, heads, own, far, cost):
    rows = own.shape[1]
    return pl.pallas_call(
        functools.partial(merge_kernel, first),
        out_shape=jax.ShapeDtypeStruct((2 * rows, heads * HD), BF16),
        in_specs=[spec_whole()] * 2,
        out_specs=spec_whole(),
        compiler_params=params(),
        cost_estimate=pl.CostEstimate(
            flops=cost, bytes_accessed=heads * rows * HD * 14, transcendentals=0
        ),
        name="merge",
    )(own, far)


def stage_kernel(groups, place, weight, *refs):
    count = (len(refs) - 1 - len(groups)) + 1
    pieces, outs, sems = refs[: count - 1], refs[count - 1 : -1], refs[-1]
    width = outs[0].shape[1] // 2
    copies = []
    for (first, heads), out in zip(groups, outs):
        tall = heads * HD
        for d in range(count):
            for half in range(2):
                start = lax.rem(place[1] + half, 2) * width
                if d == 0:
                    start = start + place[0] * (2 * width)
                source = pieces[d - 1] if d else weight
                copies.append(
                    pltpu.make_async_copy(
                        source.at[
                            pl.ds(first * HD, tall), pl.ds(pl.multiple_of(start, HD), width)
                        ],
                        out.at[pl.ds(d * tall, tall), pl.ds(half * width, width)],
                        sems.at[len(copies)],
                    )
                )
    for copy in copies:
        copy.start()
    for copy in copies:
        copy.wait()


def stage(groups, place, weight, pieces):
    depth, width = pieces[0].shape
    count = len(pieces) + 1
    return pl.pallas_call(
        functools.partial(stage_kernel, groups),
        out_shape=[jax.ShapeDtypeStruct((count * n * HD, width), BF16) for _, n in groups],
        in_specs=[pl.BlockSpec(memory_space=pltpu.SMEM)]
        + [pl.BlockSpec(memory_space=pltpu.HBM)] * count,
        out_specs=[spec_whole()] * len(groups),
        scratch_shapes=[pltpu.SemaphoreType.DMA((2 * count * len(groups),))],
        compiler_params=params(),
        cost_estimate=pl.CostEstimate(
            flops=0, bytes_accessed=4 * count * depth * width, transcendentals=0
        ),
        name="stage",
    )(place, weight, *pieces)


def project_kernel(halves, with_acc, *refs):
    refs = list(refs)
    out = refs.pop()
    acc = refs.pop() if with_acc else None
    weight = refs.pop()
    width = weight.shape[1] // 2
    step = width // 2
    left = jnp.concatenate([r[...] for r in refs], axis=1)
    for i, half in enumerate(halves):
        for j in range(2):
            columns = slice(half * width + j * step, half * width + (j + 1) * step)
            total = jnp.dot(left, weight[:, columns], preferred_element_type=F32)
            if with_acc:
                total = total + acc[:, columns]
            to = i * width + j * step
            out[:, to : to + step] = total.astype(out.dtype)


def project(atts, weight, halves, acc, dtype):
    rows = atts[0].shape[0]
    depth, width = weight.shape[0], len(halves) * weight.shape[1] // 2
    arrays = [*atts, weight] + ([] if acc is None else [acc])
    return pl.pallas_call(
        functools.partial(project_kernel, halves, acc is not None),
        out_shape=jax.ShapeDtypeStruct((rows, width), dtype),
        in_specs=[spec_whole()] * len(arrays),
        out_specs=spec_whole(),
        compiler_params=params(16),
        cost_estimate=pl.CostEstimate(
            flops=rows * width * depth,
            bytes_accessed=width * (rows * 6 + depth * 2),
            transcendentals=0,
        ),
        name="project",
    )(*arrays)


def finish_kernel(mine, other, res, res_t, gate, gate_t, out, out_t):
    rows = res.shape[0]
    projected = mine[0:rows, :] + other[0:rows, :].astype(F32)
    projected_t = mine[rows:, :] + other[rows:, :].astype(F32)
    g = gate[...]
    out[...] = (res[...].astype(F32) + g * projected).astype(out.dtype)
    out_t[...] = (res_t[...].astype(F32) + gate_t[...] * projected + g * projected_t).astype(
        out_t.dtype
    )


def finish(mine, other, res, res_t, gate, gate_t):
    rows, width = res.shape
    step = width // 2
    tall = pl.BlockSpec((2 * rows, step), lambda i: (0, i))
    short = pl.BlockSpec((rows, step), lambda i: (0, i))
    line = pl.BlockSpec((1, step), lambda i: (0, i))
    return pl.pallas_call(
        finish_kernel,
        grid=(width // step,),
        out_shape=[jax.ShapeDtypeStruct((rows, width), BF16)] * 2,
        in_specs=[tall, tall, short, short, line, line],
        out_specs=[short, short],
        compiler_params=params(),
        cost_estimate=pl.CostEstimate(flops=0, bytes_accessed=rows * width * 20, transcendentals=0),
        name="finish",
    )(mine, other, res, res_t, gate[None, :], gate_t[None, :])


def in_hbm(value):
    return pltpu.with_memory_space_constraint(value, pltpu.HBM)


def ring_pairs(size, shift):
    return [(i, (i + shift) % size) for i in range(size)]


def after(value, *others):
    return lax.optimization_barrier((value, others))[0]


def each(values, *others):
    return tuple(after(value, *others) for value in values)


def per_device(sizes, q, qt, k, kt, v, vt, residual, residual_t, weight, gate, gate_t):
    n_z, n_x = sizes
    heads = q.shape[1] // HD
    features = residual.shape[1]
    groups = [(0, 1), (1, heads - 1)]
    swap = [(0, 1), (1, 0)]
    up, down = ring_pairs(n_z, 1), ring_pairs(n_z, -1)
    q, qt, k, kt, v, vt = (in_hbm(item) for item in (q, qt, k, kt, v, vt))
    packed = pack(k, kt, v, vt)
    q_own = pack_queries(q, qt)
    q_far = lax.ppermute(q_own, "y_hi", swap)

    x = lax.axis_index("x")
    here = jnp.stack([x, lax.axis_index("core")]).astype(jnp.int32)

    def piece(d, *others):
        corner = lax.rem(x + d, n_x) * (2 * features)
        part = lax.dynamic_slice_in_dim(weight, corner, 2 * features, 1)
        return lax.ppermute(after(part, *others), "x", ring_pairs(n_x, d))

    near = [piece(1), piece(n_x - 1)]
    pieces = [near[0]] + [piece(d, *near) for d in range(2, n_x - 1)] + [near[1]]

    def hop(pair):
        return lax.ppermute(pair[0], "z", up), lax.ppermute(pair[1], "z", down)

    def turn(pair):
        return hop((pair[0][0], pair[1][1]))

    run = functools.partial(attend, q_own, q_far, groups)
    step1 = hop((packed, packed))
    step2 = hop(each(step1, q_far))
    state = run([packed, *step1])
    step3 = hop(each(step2, state, *near))
    state = run([*step2], state=state)
    step4 = turn(each(step3, state))
    state = run([*step3], state=state)
    own, *far = run([step4], state=state, final=True)
    staged = stage(groups, here, in_hbm(weight), [in_hbm(item) for item in after(pieces, own)])

    gathered, arrived = [], own
    for group, item in zip(groups, far):
        waits = (arrived, staged) if group[0] else ()
        arrived = lax.ppermute(after(item, *waits), "y_hi", swap)
        att = merge(*group, own, arrived, 10**10 if group[0] else 0)
        gathered.append(
            [att] + [lax.ppermute(att, "x", ring_pairs(n_x, d)) for d in range(1, n_x)]
        )
    acc = project(gathered[0], staged[0], (0, 1), None, F32)
    run = functools.partial(project, gathered[1], staged[1])
    to_core = run((1,), acc, BF16)
    from_core = lax.ppermute(to_core, "core", swap)
    mine = run((0,), acc, F32)
    return tuple(finish(mine, from_core, residual, residual_t, gate, gate_t))


def solution(mesh):
    n_z, n_x = mesh.shape["seq"] // 2, mesh.shape["head"] // 2
    fine = Mesh(
        mesh.devices.reshape(n_z, 2, n_x, 2, mesh.shape["dp"]), ("z", "y_hi", "x", "core", "dp")
    )
    tokens, width = ("dp", "z", "y_hi"), ("x", "core")
    wide = P(tokens, width)
    gates = P(("dp", "x", "core"))
    return jax.shard_map(
        functools.partial(per_device, (n_z, n_x)),
        mesh=fine,
        in_specs=(wide,) * 8 + (P(width, None), gates, gates),
        out_specs=(wide, wide),
        check_vma=False,
    )
```

```python
import functools

import jax
import jax.numpy as jnp
from jax import lax
from jax.experimental import pallas as pl
from jax.experimental.pallas import tpu as pltpu
from jax.sharding import Mesh
from jax.sharding import PartitionSpec as P

HD = 128
SCALE = HD ** (-0.5)
SCALE2 = SCALE * 1.4426950408889634
NT = (((1,), (1,)), ((), ()))
BF16 = jnp.bfloat16
F32 = jnp.float32
STATS = 8


def spec_whole():
    return pl.BlockSpec(memory_space=pltpu.VMEM)


def params(mib=12):
    return pltpu.CompilerParams(vmem_limit_bytes=mib * 1024 * 1024)


def query_kernel(q, qt, out, sems):
    copies = []
    for h in range(q.shape[1] // HD):
        for i, ref in enumerate((qt, q)):
            copies.append(
                pltpu.make_async_copy(
                    ref.at[:, h * HD : (h + 1) * HD],
                    out.at[:, (2 * h + i) * HD : (2 * h + i + 1) * HD],
                    sems.at[2 * h + i],
                )
            )
    for copy in copies:
        copy.start()
    for copy in copies:
        copy.wait()


def pack_queries(q, qt):
    rows, width = q.shape
    return pl.pallas_call(
        query_kernel,
        out_shape=jax.ShapeDtypeStruct((rows, 2 * width), BF16),
        in_specs=[pl.BlockSpec(memory_space=pltpu.HBM)] * 2,
        out_specs=spec_whole(),
        scratch_shapes=[pltpu.SemaphoreType.DMA((2 * width // HD,))],
        compiler_params=params(),
        cost_estimate=pl.CostEstimate(flops=0, bytes_accessed=8 * rows * width, transcendentals=0),
        name="pack_queries",
    )(q, qt)


def pack_kernel(k, kt, v, vt, out, scratch, sems):
    heads = k.shape[1] // HD
    values = [
        pltpu.make_async_copy(ref, scratch.at[i], sems.at[2 * heads + i])
        for i, ref in enumerate((v, vt))
    ]
    copies = []
    for h in range(heads):
        for i, ref in enumerate((k, kt)):
            copies.append(
                pltpu.make_async_copy(
                    ref.at[:, h * HD : (h + 1) * HD],
                    out.at[0, 2 * h * HD : 2 * (h + 1) * HD, i * HD : (i + 1) * HD],
                    sems.at[2 * h + i],
                )
            )
    for copy in values + copies:
        copy.start()
    for i, copy in enumerate(values):
        copy.wait()
        for h in range(heads):
            part = scratch[i, :, h * HD : (h + 1) * HD].T
            out[1, (2 * h + i) * HD : (2 * h + i + 1) * HD, :] = part
    for copy in copies:
        copy.wait()


def pack(k, kt, v, vt):
    rows, width = k.shape
    return pl.pallas_call(
        pack_kernel,
        out_shape=jax.ShapeDtypeStruct((2, 2 * width, rows), BF16),
        in_specs=[pl.BlockSpec(memory_space=pltpu.HBM)] * 4,
        out_specs=spec_whole(),
        scratch_shapes=[
            pltpu.VMEM((2, rows, width), BF16),
            pltpu.SemaphoreType.DMA((2 * width // HD + 2,)),
        ],
        compiler_params=params(),
        cost_estimate=pl.CostEstimate(flops=0, bytes_accessed=16 * rows * width, transcendentals=0),
        name="pack",
    )(k, kt, v, vt)


def three_parts(value):
    high = value.astype(BF16)
    rest = value - high.astype(F32)
    middle = rest.astype(BF16)
    low = (rest - middle.astype(F32)).astype(BF16)
    return [high, middle, low]


def attend_kernel(kinds, groups, with_state, final, *refs):
    refs = list(refs)
    scores_ref = refs.pop()
    q_refs = [refs.pop(0), refs.pop(0)]
    pairs = []
    for halves in kinds:
        if halves:
            pairs.append((refs.pop(0), refs.pop(0)))
        else:
            both = refs.pop(0)
            pairs.append((both.at[0], both.at[1]))
    state = refs.pop(0) if with_state else None
    keys = q_refs[0].shape[0]
    tall, far_tall = 2 * HD + STATS, 2 * HD + 2 * STATS
    where = [(g, i) for g, (_, count) in enumerate(groups) for i in range(count)]
    for h, (group, inner) in enumerate(where):
        place = pl.ds(2 * h * HD, 2 * HD)
        q2 = jnp.concatenate([r[:, place] for r in q_refs], axis=0)
        old = state.at[pl.ds(h * tall, tall), :] if with_state else None
        sums = attend_blocks(
            q2, [(k.at[place, :], v.at[place, :]) for k, v in pairs], old, scores_ref
        )
        acc_out, acc_tan, top, total, mixed_sum = sums
        if not final:
            put(refs[0], h * tall, *sums)
            continue
        inverse = 1.0 / total
        ratio = mixed_sum * inverse
        attention = acc_out * inverse
        attention_t = acc_tan * inverse - ratio * attention
        parts = (attention, attention_t, top, total, ratio)
        own, far = refs[0], refs[1 + group]
        put(own, h * tall, *(p[:, :keys] for p in parts))
        base = inner * far_tall
        far[base : base + HD, :] = attention[:, keys:].astype(BF16)
        far[base + HD : base + 2 * HD, :] = attention_t[:, keys:].astype(BF16)
        stats = three_parts(top) + three_parts(total) + three_parts(ratio)
        stats = [s[:, keys:].astype(F32) for s in stats]
        stats.append(jnp.zeros((2 * STATS - len(stats), keys), F32))
        far[base + 2 * HD : base + far_tall, :] = jnp.concatenate(stats, axis=0).astype(BF16)


def put(out, base, upper, lower, *lines):
    out[base : base + HD, :] = upper
    out[base + HD : base + 2 * HD, :] = lower
    for i, line in enumerate(lines):
        out[base + 2 * HD + i : base + 2 * HD + i + 1, :] = line


def attend_blocks(q2, pairs, state, scores_ref):
    rows = q2.shape[0]
    keys = rows // 2
    q = q2[:, HD:]
    top = state[2 * HD : 2 * HD + 1, :] if state is not None else None
    old_top = top
    for i, (k_ref, _) in enumerate(pairs):
        scores = lax.dot_general(k_ref[:, 0:HD], q, NT, preferred_element_type=F32)
        scores_ref[i * keys : (i + 1) * keys, :] = scores
        peak = jnp.max(scores, axis=0, keepdims=True) * SCALE2
        top = peak if top is None else jnp.maximum(top, peak)
    total = jnp.zeros((1, rows), F32)
    mixed_sum = jnp.zeros((1, rows), F32)
    all_weights, all_mixed = [], []
    for i, (k_ref, _) in enumerate(pairs):
        tangent = lax.dot_general(k_ref[...], q2, NT, preferred_element_type=F32)
        weights = jnp.exp2(scores_ref[i * keys : (i + 1) * keys, :] * SCALE2 - top)
        mixed = weights * tangent
        total = total + jnp.sum(weights, axis=0, keepdims=True)
        mixed_sum = mixed_sum + jnp.sum(mixed, axis=0, keepdims=True)
        all_weights.append(weights.astype(BF16))
        all_mixed.append(mixed.astype(BF16))
    values = jnp.concatenate([v_ref[...] for _, v_ref in pairs], axis=1)
    acc = jnp.dot(values, jnp.concatenate(all_weights, axis=0), preferred_element_type=F32)
    acc_mixed = jnp.dot(
        values[0:HD, :], jnp.concatenate(all_mixed, axis=0), preferred_element_type=F32
    )
    acc_out = acc[0:HD, :]
    acc_tan = acc[HD:, :] + SCALE * acc_mixed
    mixed_sum = SCALE * mixed_sum
    if state is not None:
        shrink = jnp.exp2(old_top - top)
        acc_out = acc_out + shrink * state[0:HD, :]
        acc_tan = acc_tan + shrink * state[HD : 2 * HD, :]
        total = total + shrink * state[2 * HD + 1 : 2 * HD + 2, :]
        mixed_sum = mixed_sum + shrink * state[2 * HD + 2 : 2 * HD + 3, :]
    return acc_out, acc_tan, top, total, mixed_sum


def attend(q_own, q_far, groups, blocks, state=None, final=False):
    rows = q_own.shape[0]
    heads = sum(count for _, count in groups)
    n = len(blocks)
    tall, far = 2 * HD + STATS, 2 * HD + 2 * STATS
    kinds = [isinstance(block, tuple) for block in blocks]
    arrays = [q_own, q_far]
    for block in blocks:
        arrays.extend(block if isinstance(block, tuple) else (block,))
    if state is not None:
        arrays.append(state)
    if final:
        outs = [
            jax.ShapeDtypeStruct((heads * tall, rows), F32),
            *(jax.ShapeDtypeStruct((count * far, rows), BF16) for _, count in groups),
        ]
    else:
        outs = [jax.ShapeDtypeStruct((heads * tall, 2 * rows), F32)]
    result = pl.pallas_call(
        functools.partial(attend_kernel, kinds, groups, state is not None, final),
        out_shape=outs,
        in_specs=[spec_whole()] * len(arrays),
        out_specs=[spec_whole()] * len(outs),
        scratch_shapes=[pltpu.VMEM((n * rows, 2 * rows), F32)],
        compiler_params=params(8),
        cost_estimate=pl.CostEstimate(
            flops=4 * heads * 2 * 2 * rows * n * rows * HD * 8,
            bytes_accessed=heads * 2 * rows * HD * 4 * (n + 2),
            transcendentals=heads * 2 * rows * n * rows,
        ),
        name="attend",
    )(*arrays)
    return result if final else result[0]


def merge_kernel(first, own_ref, far_ref, out):
    rows = own_ref.shape[1]
    tall, far_tall = 2 * HD + STATS, 2 * HD + 2 * STATS
    for h in range(far_ref.shape[0] // far_tall):
        own = own_ref[(first + h) * tall : (first + h + 1) * tall, :]
        far = far_ref[h * far_tall : (h + 1) * far_tall, :]
        attention, tangent = merge_parts(own, far)
        out[0:rows, h * HD : (h + 1) * HD] = attention.T.astype(BF16)
        out[rows:, h * HD : (h + 1) * HD] = tangent.T.astype(BF16)


def merge_parts(own, far):
    stats = far[2 * HD :, :].astype(F32)
    pick = lambda i: stats[3 * i : 3 * i + 1] + stats[3 * i + 1 : 3 * i + 2] + stats[3 * i + 2 : 3 * i + 3]
    top0, total0, ratio0 = (own[2 * HD + i : 2 * HD + i + 1, :] for i in range(3))
    top1, total1, ratio1 = pick(0), pick(1), pick(2)
    top = jnp.maximum(top0, top1)
    part0 = total0 * jnp.exp2(top0 - top)
    part1 = total1 * jnp.exp2(top1 - top)
    inverse = 1.0 / (part0 + part1)
    part0, part1 = part0 * inverse, part1 * inverse
    att0, att1 = own[0:HD, :], far[0:HD, :].astype(F32)
    tan0, tan1 = own[HD : 2 * HD, :], far[HD : 2 * HD, :].astype(F32)
    attention = part0 * att0 + part1 * att1
    tangent = part0 * tan0 + part1 * tan1 + (part0 * part1 * (ratio0 - ratio1)) * (att0 - att1)
    return attention, tangent


def merge(first, heads, own, far, cost):
    rows = own.shape[1]
    return pl.pallas_call(
        functools.partial(merge_kernel, first),
        out_shape=jax.ShapeDtypeStruct((2 * rows, heads * HD), BF16),
        in_specs=[spec_whole()] * 2,
        out_specs=spec_whole(),
        compiler_params=params(),
        cost_estimate=pl.CostEstimate(
            flops=cost, bytes_accessed=heads * rows * HD * 14, transcendentals=0
        ),
        name="merge",
    )(own, far)


def stage_kernel(groups, place, weight, *refs):
    count = (len(refs) - 1 - len(groups)) + 1
    pieces, outs, sems = refs[: count - 1], refs[count - 1 : -1], refs[-1]
    width = outs[0].shape[1] // 2
    copies = []
    for (first, heads), out in zip(groups, outs):
        tall = heads * HD
        for d in range(count):
            for half in range(2):
                start = lax.rem(place[1] + half, 2) * width
                if d == 0:
                    start = start + place[0] * (2 * width)
                source = pieces[d - 1] if d else weight
                copies.append(
                    pltpu.make_async_copy(
                        source.at[
                            pl.ds(first * HD, tall), pl.ds(pl.multiple_of(start, HD), width)
                        ],
                        out.at[pl.ds(d * tall, tall), pl.ds(half * width, width)],
                        sems.at[len(copies)],
                    )
                )
    for copy in copies:
        copy.start()
    for copy in copies:
        copy.wait()


def stage(groups, place, weight, pieces):
    depth, width = pieces[0].shape
    count = len(pieces) + 1
    return pl.pallas_call(
        functools.partial(stage_kernel, groups),
        out_shape=[jax.ShapeDtypeStruct((count * n * HD, width), BF16) for _, n in groups],
        in_specs=[pl.BlockSpec(memory_space=pltpu.SMEM)]
        + [pl.BlockSpec(memory_space=pl.ANY)] * count,
        out_specs=[spec_whole()] * len(groups),
        scratch_shapes=[pltpu.SemaphoreType.DMA((2 * count * len(groups),))],
        compiler_params=params(),
        cost_estimate=pl.CostEstimate(
            flops=0, bytes_accessed=4 * count * depth * width, transcendentals=0
        ),
        name="stage",
    )(place, weight, *pieces)


def project_kernel(halves, with_acc, *refs):
    refs = list(refs)
    out = refs.pop()
    acc = refs.pop() if with_acc else None
    weight = refs.pop()
    width = weight.shape[1] // 2
    step = width // 2
    left = jnp.concatenate([r[...] for r in refs], axis=1)
    for i, half in enumerate(halves):
        for j in range(2):
            columns = slice(half * width + j * step, half * width + (j + 1) * step)
            total = jnp.dot(left, weight[:, columns], preferred_element_type=F32)
            if with_acc:
                total = total + acc[:, columns]
            to = i * width + j * step
            out[:, to : to + step] = total.astype(out.dtype)


def project(atts, weight, halves, acc, dtype, cost=0):
    rows = atts[0].shape[0]
    depth, width = weight.shape[0], len(halves) * weight.shape[1] // 2
    arrays = [*atts, weight] + ([] if acc is None else [acc])
    return pl.pallas_call(
        functools.partial(project_kernel, halves, acc is not None),
        out_shape=jax.ShapeDtypeStruct((rows, width), dtype),
        in_specs=[spec_whole()] * len(arrays),
        out_specs=spec_whole(),
        compiler_params=params(16),
        cost_estimate=pl.CostEstimate(
            flops=max(cost, rows * width * depth),
            bytes_accessed=width * (rows * 6 + depth * 2),
            transcendentals=0,
        ),
        name="project",
    )(*arrays)


def finish_kernel(mine, other, res, res_t, gate, gate_t, out, out_t):
    rows = res.shape[0]
    projected = mine[0:rows, :] + other[0:rows, :].astype(F32)
    projected_t = mine[rows:, :] + other[rows:, :].astype(F32)
    g = gate[...]
    out[...] = (res[...].astype(F32) + g * projected).astype(out.dtype)
    out_t[...] = (res_t[...].astype(F32) + gate_t[...] * projected + g * projected_t).astype(
        out_t.dtype
    )


def finish(mine, other, res, res_t, gate, gate_t):
    rows, width = res.shape
    step = width // 2
    tall = pl.BlockSpec((2 * rows, step), lambda i: (0, i))
    short = pl.BlockSpec((rows, step), lambda i: (0, i))
    line = pl.BlockSpec((1, step), lambda i: (0, i))
    return pl.pallas_call(
        finish_kernel,
        grid=(width // step,),
        out_shape=[jax.ShapeDtypeStruct((rows, width), BF16)] * 2,
        in_specs=[tall, tall, short, short, line, line],
        out_specs=[short, short],
        compiler_params=params(),
        cost_estimate=pl.CostEstimate(flops=0, bytes_accessed=rows * width * 20, transcendentals=0),
        name="finish",
    )(mine, other, res, res_t, gate[None, :], gate_t[None, :])


def in_hbm(value):
    return pltpu.with_memory_space_constraint(value, pltpu.HBM)


def ring_pairs(size, shift):
    return [(i, (i + shift) % size) for i in range(size)]


def after(value, *others):
    return lax.optimization_barrier((value, others))[0]


def each(values, *others):
    return tuple(after(value, *others) for value in values)


def per_device(sizes, q, qt, k, kt, v, vt, residual, residual_t, weight, gate, gate_t):
    n_z, n_x = sizes
    heads = q.shape[1] // HD
    features = residual.shape[1]
    groups = [(0, 1), (1, heads - 1)]
    swap = [(0, 1), (1, 0)]
    up, down = ring_pairs(n_z, 1), ring_pairs(n_z, -1)
    q, qt, k, kt, v, vt = (in_hbm(item) for item in (q, qt, k, kt, v, vt))
    packed = pack(k, kt, v, vt)
    q_own = pack_queries(q, qt)
    q_far = lax.ppermute(q_own, "y_hi", swap)

    x = lax.axis_index("x")
    here = jnp.stack([x, lax.axis_index("core")]).astype(jnp.int32)

    def piece(d, *others):
        corner = lax.rem(x + d, n_x) * (2 * features)
        part = lax.dynamic_slice_in_dim(weight, corner, 2 * features, 1)
        return lax.ppermute(after(part, *others), "x", ring_pairs(n_x, d))

    near = [piece(1), piece(n_x - 1)]

    def hop(pair):
        return lax.ppermute(pair[0], "z", up), lax.ppermute(pair[1], "z", down)

    def turn(pair):
        return hop((pair[0][0], pair[1][1]))

    run = functools.partial(attend, q_own, q_far, groups)
    step1 = hop((packed, packed))
    step2 = hop(each(step1, q_far))
    state = run([packed, *step1])
    step3 = hop(each(step2, state, *near))
    state = run([*step2], state=state)
    far_pieces = [piece(d, *near, state) for d in range(2, n_x - 1)]
    pieces = [near[0], *far_pieces, near[1]]
    step4 = turn(each(step3, state))
    state = run([*step3], state=state)
    own, *far = run([step4], state=state, final=True)
    staged = stage(groups, here, in_hbm(weight), [in_hbm(item) for item in after(pieces, own)])
    arrived = [lax.ppermute(item, "y_hi", swap) for item in far]
    arrived[0] = after(arrived[0], staged)
    gathered = []
    for group, item in zip(groups, arrived):
        att = merge(*group, own, item, 10**10 if group[0] else 0)
        gathered.append(
            [att] + [lax.ppermute(att, "x", ring_pairs(n_x, d)) for d in range(1, n_x)]
        )
    acc = project(gathered[0], staged[0], (0, 1), None, F32, 10**10)
    run = functools.partial(project, gathered[1], staged[1])
    to_core = run((1,), acc, BF16)
    from_core = lax.ppermute(to_core, "core", swap)
    mine = run((0,), acc, F32)
    return tuple(finish(mine, from_core, residual, residual_t, gate, gate_t))


def solution(mesh):
    n_z, n_x = mesh.shape["seq"] // 2, mesh.shape["head"] // 2
    fine = Mesh(
        mesh.devices.reshape(n_z, 2, n_x, 2, mesh.shape["dp"]), ("z", "y_hi", "x", "core", "dp")
    )
    tokens, width = ("dp", "z", "y_hi"), ("x", "core")
    wide = P(tokens, width)
    gates = P(("dp", "x", "core"))
    return jax.shard_map(
        functools.partial(per_device, (n_z, n_x)),
        mesh=fine,
        in_specs=(wide,) * 8 + (P(width, None), gates, gates),
        out_specs=(wide, wide),
        check_vma=False,
    )
```

```python
import functools

import jax
import jax.numpy as jnp
from jax import lax
from jax.experimental import pallas as pl
from jax.experimental.pallas import tpu as pltpu
from jax.sharding import Mesh
from jax.sharding import PartitionSpec as P

HD = 128
SCALE = HD ** (-0.5)
SCALE2 = SCALE * 1.4426950408889634
NT = (((1,), (1,)), ((), ()))
BF16 = jnp.bfloat16
F32 = jnp.float32
STATS = 8


def spec_whole():
    return pl.BlockSpec(memory_space=pltpu.VMEM)


def params(mib=12):
    return pltpu.CompilerParams(vmem_limit_bytes=mib * 1024 * 1024)


def query_kernel(q, qt, out, sems):
    copies = []
    for h in range(q.shape[1] // HD):
        for i, ref in enumerate((qt, q)):
            copies.append(
                pltpu.make_async_copy(
                    ref.at[:, h * HD : (h + 1) * HD],
                    out.at[:, (2 * h + i) * HD : (2 * h + i + 1) * HD],
                    sems.at[2 * h + i],
                )
            )
    for copy in copies:
        copy.start()
    for copy in copies:
        copy.wait()


def pack_queries(q, qt):
    rows, width = q.shape
    return pl.pallas_call(
        query_kernel,
        out_shape=jax.ShapeDtypeStruct((rows, 2 * width), BF16),
        in_specs=[pl.BlockSpec(memory_space=pltpu.HBM)] * 2,
        out_specs=spec_whole(),
        scratch_shapes=[pltpu.SemaphoreType.DMA((2 * width // HD,))],
        compiler_params=params(),
        cost_estimate=pl.CostEstimate(flops=0, bytes_accessed=8 * rows * width, transcendentals=0),
        name="pack_queries",
    )(q, qt)


def pack_kernel(k, kt, v, vt, out, scratch, sems):
    heads = k.shape[1] // HD
    values = [
        pltpu.make_async_copy(ref, scratch.at[i], sems.at[2 * heads + i])
        for i, ref in enumerate((v, vt))
    ]
    copies = []
    for h in range(heads):
        for i, ref in enumerate((k, kt)):
            copies.append(
                pltpu.make_async_copy(
                    ref.at[:, h * HD : (h + 1) * HD],
                    out.at[0, 2 * h * HD : 2 * (h + 1) * HD, i * HD : (i + 1) * HD],
                    sems.at[2 * h + i],
                )
            )
    for copy in values + copies:
        copy.start()
    for i, copy in enumerate(values):
        copy.wait()
        for h in range(heads):
            part = scratch[i, :, h * HD : (h + 1) * HD].T
            out[1, (2 * h + i) * HD : (2 * h + i + 1) * HD, :] = part
    for copy in copies:
        copy.wait()


def pack(k, kt, v, vt):
    rows, width = k.shape
    return pl.pallas_call(
        pack_kernel,
        out_shape=jax.ShapeDtypeStruct((2, 2 * width, rows), BF16),
        in_specs=[pl.BlockSpec(memory_space=pltpu.HBM)] * 4,
        out_specs=spec_whole(),
        scratch_shapes=[
            pltpu.VMEM((2, rows, width), BF16),
            pltpu.SemaphoreType.DMA((2 * width // HD + 2,)),
        ],
        compiler_params=params(),
        cost_estimate=pl.CostEstimate(flops=0, bytes_accessed=16 * rows * width, transcendentals=0),
        name="pack",
    )(k, kt, v, vt)


def three_parts(value):
    high = value.astype(BF16)
    rest = value - high.astype(F32)
    middle = rest.astype(BF16)
    low = (rest - middle.astype(F32)).astype(BF16)
    return [high, middle, low]


def attend_kernel(kinds, groups, with_state, final, *refs):
    refs = list(refs)
    scores_ref = refs.pop()
    q_refs = [refs.pop(0), refs.pop(0)]
    pairs = []
    for halves in kinds:
        if halves:
            pairs.append((refs.pop(0), refs.pop(0)))
        else:
            both = refs.pop(0)
            pairs.append((both.at[0], both.at[1]))
    state = refs.pop(0) if with_state else None
    keys = q_refs[0].shape[0]
    tall, far_tall = 2 * HD + STATS, 2 * HD + 2 * STATS
    where = [(g, i) for g, (_, count) in enumerate(groups) for i in range(count)]
    for h, (group, inner) in enumerate(where):
        place = pl.ds(2 * h * HD, 2 * HD)
        q2 = jnp.concatenate([r[:, place] for r in q_refs], axis=0)
        old = state.at[pl.ds(h * tall, tall), :] if with_state else None
        sums = attend_blocks(
            q2, [(k.at[place, :], v.at[place, :]) for k, v in pairs], old, scores_ref
        )
        acc_out, acc_tan, top, total, mixed_sum = sums
        if not final:
            put(refs[0], h * tall, *sums)
            continue
        inverse = 1.0 / total
        ratio = mixed_sum * inverse
        attention = acc_out * inverse
        attention_t = acc_tan * inverse - ratio * attention
        parts = (attention, attention_t, top, total, ratio)
        own, far = refs[0], refs[1 + group]
        put(own, h * tall, *(p[:, :keys] for p in parts))
        base = inner * far_tall
        far[base : base + HD, :] = attention[:, keys:].astype(BF16)
        far[base + HD : base + 2 * HD, :] = attention_t[:, keys:].astype(BF16)
        stats = three_parts(top) + three_parts(total) + three_parts(ratio)
        stats = [s[:, keys:].astype(F32) for s in stats]
        stats.append(jnp.zeros((2 * STATS - len(stats), keys), F32))
        far[base + 2 * HD : base + far_tall, :] = jnp.concatenate(stats, axis=0).astype(BF16)


def put(out, base, upper, lower, *lines):
    out[base : base + HD, :] = upper
    out[base + HD : base + 2 * HD, :] = lower
    for i, line in enumerate(lines):
        out[base + 2 * HD + i : base + 2 * HD + i + 1, :] = line


def attend_blocks(q2, pairs, state, scores_ref):
    rows = q2.shape[0]
    keys = rows // 2
    q = q2[:, HD:]
    top = state[2 * HD : 2 * HD + 1, :] if state is not None else None
    old_top = top
    for i, (k_ref, _) in enumerate(pairs):
        scores = lax.dot_general(k_ref[:, 0:HD], q, NT, preferred_element_type=F32)
        scores_ref[i * keys : (i + 1) * keys, :] = scores
        peak = jnp.max(scores, axis=0, keepdims=True) * SCALE2
        top = peak if top is None else jnp.maximum(top, peak)
    total = jnp.zeros((1, rows), F32)
    mixed_sum = jnp.zeros((1, rows), F32)
    all_weights, all_mixed = [], []
    for i, (k_ref, _) in enumerate(pairs):
        tangent = lax.dot_general(k_ref[...], q2, NT, preferred_element_type=F32)
        weights = jnp.exp2(scores_ref[i * keys : (i + 1) * keys, :] * SCALE2 - top)
        mixed = weights * tangent
        total = total + jnp.sum(weights, axis=0, keepdims=True)
        mixed_sum = mixed_sum + jnp.sum(mixed, axis=0, keepdims=True)
        all_weights.append(weights.astype(BF16))
        all_mixed.append(mixed.astype(BF16))
    values = jnp.concatenate([v_ref[...] for _, v_ref in pairs], axis=1)
    acc = jnp.dot(values, jnp.concatenate(all_weights, axis=0), preferred_element_type=F32)
    acc_mixed = jnp.dot(
        values[0:HD, :], jnp.concatenate(all_mixed, axis=0), preferred_element_type=F32
    )
    acc_out = acc[0:HD, :]
    acc_tan = acc[HD:, :] + SCALE * acc_mixed
    mixed_sum = SCALE * mixed_sum
    if state is not None:
        shrink = jnp.exp2(old_top - top)
        acc_out = acc_out + shrink * state[0:HD, :]
        acc_tan = acc_tan + shrink * state[HD : 2 * HD, :]
        total = total + shrink * state[2 * HD + 1 : 2 * HD + 2, :]
        mixed_sum = mixed_sum + shrink * state[2 * HD + 2 : 2 * HD + 3, :]
    return acc_out, acc_tan, top, total, mixed_sum


def attend(q_own, q_far, groups, blocks, state=None, final=False):
    rows = q_own.shape[0]
    heads = sum(count for _, count in groups)
    n = len(blocks)
    tall, far = 2 * HD + STATS, 2 * HD + 2 * STATS
    kinds = [isinstance(block, tuple) for block in blocks]
    arrays = [q_own, q_far]
    for block in blocks:
        arrays.extend(block if isinstance(block, tuple) else (block,))
    if state is not None:
        arrays.append(state)
    if final:
        outs = [
            jax.ShapeDtypeStruct((heads * tall, rows), F32),
            *(jax.ShapeDtypeStruct((count * far, rows), BF16) for _, count in groups),
        ]
    else:
        outs = [jax.ShapeDtypeStruct((heads * tall, 2 * rows), F32)]
    result = pl.pallas_call(
        functools.partial(attend_kernel, kinds, groups, state is not None, final),
        out_shape=outs,
        in_specs=[spec_whole()] * len(arrays),
        out_specs=[spec_whole()] * len(outs),
        scratch_shapes=[pltpu.VMEM((n * rows, 2 * rows), F32)],
        compiler_params=params(8),
        cost_estimate=pl.CostEstimate(
            flops=4 * heads * 2 * 2 * rows * n * rows * HD * 8,
            bytes_accessed=heads * 2 * rows * HD * 4 * (n + 2),
            transcendentals=heads * 2 * rows * n * rows,
        ),
        name="attend",
    )(*arrays)
    return result if final else result[0]


def merge_kernel(first, own_ref, far_ref, out):
    rows = own_ref.shape[1]
    tall, far_tall = 2 * HD + STATS, 2 * HD + 2 * STATS
    for h in range(far_ref.shape[0] // far_tall):
        own = own_ref[(first + h) * tall : (first + h + 1) * tall, :]
        far = far_ref[h * far_tall : (h + 1) * far_tall, :]
        attention, tangent = merge_parts(own, far)
        out[0:rows, h * HD : (h + 1) * HD] = attention.T.astype(BF16)
        out[rows:, h * HD : (h + 1) * HD] = tangent.T.astype(BF16)


def merge_parts(own, far):
    stats = far[2 * HD :, :].astype(F32)
    pick = lambda i: stats[3 * i : 3 * i + 1] + stats[3 * i + 1 : 3 * i + 2] + stats[3 * i + 2 : 3 * i + 3]
    top0, total0, ratio0 = (own[2 * HD + i : 2 * HD + i + 1, :] for i in range(3))
    top1, total1, ratio1 = pick(0), pick(1), pick(2)
    top = jnp.maximum(top0, top1)
    part0 = total0 * jnp.exp2(top0 - top)
    part1 = total1 * jnp.exp2(top1 - top)
    inverse = 1.0 / (part0 + part1)
    part0, part1 = part0 * inverse, part1 * inverse
    att0, att1 = own[0:HD, :], far[0:HD, :].astype(F32)
    tan0, tan1 = own[HD : 2 * HD, :], far[HD : 2 * HD, :].astype(F32)
    attention = part0 * att0 + part1 * att1
    tangent = part0 * tan0 + part1 * tan1 + (part0 * part1 * (ratio0 - ratio1)) * (att0 - att1)
    return attention, tangent


def merge(first, heads, own, far, cost):
    rows = own.shape[1]
    return pl.pallas_call(
        functools.partial(merge_kernel, first),
        out_shape=jax.ShapeDtypeStruct((2 * rows, heads * HD), BF16),
        in_specs=[spec_whole()] * 2,
        out_specs=spec_whole(),
        compiler_params=params(),
        cost_estimate=pl.CostEstimate(
            flops=cost, bytes_accessed=heads * rows * HD * 14, transcendentals=0
        ),
        name="merge",
    )(own, far)


def stage_kernel(groups, place, weight, *refs):
    count = (len(refs) - 1 - len(groups)) + 1
    pieces, outs, sems = refs[: count - 1], refs[count - 1 : -1], refs[-1]
    width = outs[0].shape[1] // 2
    copies = []
    for (first, heads), out in zip(groups, outs):
        tall = heads * HD
        for d in range(count):
            for half in range(2):
                start = lax.rem(place[1] + half, 2) * width
                if d == 0:
                    start = start + place[0] * (2 * width)
                source = pieces[d - 1] if d else weight
                copies.append(
                    pltpu.make_async_copy(
                        source.at[
                            pl.ds(first * HD, tall), pl.ds(pl.multiple_of(start, HD), width)
                        ],
                        out.at[pl.ds(d * tall, tall), pl.ds(half * width, width)],
                        sems.at[len(copies)],
                    )
                )
    for copy in copies:
        copy.start()
    for copy in copies:
        copy.wait()


def stage(groups, place, weight, pieces):
    depth, width = pieces[0].shape
    count = len(pieces) + 1
    return pl.pallas_call(
        functools.partial(stage_kernel, groups),
        out_shape=[jax.ShapeDtypeStruct((count * n * HD, width), BF16) for _, n in groups],
        in_specs=[pl.BlockSpec(memory_space=pltpu.SMEM)]
        + [pl.BlockSpec(memory_space=pl.ANY)] * count,
        out_specs=[spec_whole()] * len(groups),
        scratch_shapes=[pltpu.SemaphoreType.DMA((2 * count * len(groups),))],
        compiler_params=params(),
        cost_estimate=pl.CostEstimate(
            flops=0, bytes_accessed=4 * count * depth * width, transcendentals=0
        ),
        name="stage",
    )(place, weight, *pieces)


def project_kernel(halves, with_acc, *refs):
    refs = list(refs)
    out = refs.pop()
    acc = refs.pop() if with_acc else None
    weight = refs.pop()
    width = weight.shape[1] // 2
    step = width // 2
    left = jnp.concatenate([r[...] for r in refs], axis=1)
    for i, half in enumerate(halves):
        for j in range(2):
            columns = slice(half * width + j * step, half * width + (j + 1) * step)
            total = jnp.dot(left, weight[:, columns], preferred_element_type=F32)
            if with_acc:
                total = total + acc[:, columns]
            to = i * width + j * step
            out[:, to : to + step] = total.astype(out.dtype)


def project(atts, weight, halves, acc, dtype, cost=0):
    rows = atts[0].shape[0]
    depth, width = weight.shape[0], len(halves) * weight.shape[1] // 2
    arrays = [*atts, weight] + ([] if acc is None else [acc])
    return pl.pallas_call(
        functools.partial(project_kernel, halves, acc is not None),
        out_shape=jax.ShapeDtypeStruct((rows, width), dtype),
        in_specs=[spec_whole()] * len(arrays),
        out_specs=spec_whole(),
        compiler_params=params(16),
        cost_estimate=pl.CostEstimate(
            flops=max(cost, rows * width * depth),
            bytes_accessed=width * (rows * 6 + depth * 2),
            transcendentals=0,
        ),
        name="project",
    )(*arrays)


def finish_kernel(mine, other, res, res_t, gate, gate_t, out, out_t):
    rows = res.shape[0]
    projected = mine[0:rows, :] + other[0:rows, :].astype(F32)
    projected_t = mine[rows:, :] + other[rows:, :].astype(F32)
    g = gate[...]
    out[...] = (res[...].astype(F32) + g * projected).astype(out.dtype)
    out_t[...] = (res_t[...].astype(F32) + gate_t[...] * projected + g * projected_t).astype(
        out_t.dtype
    )


def finish(mine, other, res, res_t, gate, gate_t):
    rows, width = res.shape
    step = width // 2
    tall = pl.BlockSpec((2 * rows, step), lambda i: (0, i))
    short = pl.BlockSpec((rows, step), lambda i: (0, i))
    line = pl.BlockSpec((1, step), lambda i: (0, i))
    return pl.pallas_call(
        finish_kernel,
        grid=(width // step,),
        out_shape=[jax.ShapeDtypeStruct((rows, width), BF16)] * 2,
        in_specs=[tall, tall, short, short, line, line],
        out_specs=[short, short],
        compiler_params=params(),
        cost_estimate=pl.CostEstimate(flops=0, bytes_accessed=rows * width * 20, transcendentals=0),
        name="finish",
    )(mine, other, res, res_t, gate[None, :], gate_t[None, :])


def in_hbm(value):
    return pltpu.with_memory_space_constraint(value, pltpu.HBM)


def ring_pairs(size, shift):
    return [(i, (i + shift) % size) for i in range(size)]


def after(value, *others):
    return lax.optimization_barrier((value, others))[0]


def each(values, *others):
    return tuple(after(value, *others) for value in values)


def per_device(sizes, q, qt, k, kt, v, vt, residual, residual_t, weight, gate, gate_t):
    n_z, n_x = sizes
    heads = q.shape[1] // HD
    features = residual.shape[1]
    groups = [(0, heads - 1), (heads - 1, 1)]
    swap = [(0, 1), (1, 0)]
    up, down = ring_pairs(n_z, 1), ring_pairs(n_z, -1)
    q, qt, k, kt, v, vt = (in_hbm(item) for item in (q, qt, k, kt, v, vt))
    packed = pack(k, kt, v, vt)
    q_own = pack_queries(q, qt)
    q_far = lax.ppermute(q_own, "y_hi", swap)

    x = lax.axis_index("x")
    here = jnp.stack([x, lax.axis_index("core")]).astype(jnp.int32)

    def piece(d, *others):
        corner = lax.rem(x + d, n_x) * (2 * features)
        part = lax.dynamic_slice_in_dim(weight, corner, 2 * features, 1)
        return lax.ppermute(after(part, *others), "x", ring_pairs(n_x, d))

    near = [piece(1), piece(n_x - 1)]

    def hop(pair):
        return lax.ppermute(pair[0], "z", up), lax.ppermute(pair[1], "z", down)

    def turn(pair):
        return hop((pair[0][0], pair[1][1]))

    run = functools.partial(attend, q_own, q_far, groups)
    step1 = hop((packed, packed))
    step2 = hop(each(step1, q_far))
    state = run([packed, *step1])
    step3 = hop(each(step2, state, *near))
    state = run([*step2], state=state)
    far_pieces = [piece(d, *near, state) for d in range(2, n_x - 1)]
    pieces = [near[0], *far_pieces, near[1]]
    step4 = turn(each(step3, state))
    state = run([*step3], state=state)
    own, *far = run([step4], state=state, final=True)
    staged = stage(groups, here, in_hbm(weight), [in_hbm(item) for item in after(pieces, own)])
    arrived = [lax.ppermute(item, "y_hi", swap) for item in far]
    arrived[0] = after(arrived[0], staged)
    gathered = []
    for group, item in zip(groups, arrived):
        att = merge(*group, own, item, 10**10 if group[0] else 0)
        gathered.append(
            [att] + [lax.ppermute(att, "x", ring_pairs(n_x, d)) for d in range(1, n_x)]
        )
    acc = project(gathered[0], staged[0], (0, 1), None, F32, 10**10)
    run = functools.partial(project, gathered[1], staged[1])
    to_core = run((1,), acc, BF16)
    from_core = lax.ppermute(to_core, "core", swap)
    mine = run((0,), acc, F32)
    return tuple(finish(mine, from_core, residual, residual_t, gate, gate_t))


def solution(mesh):
    n_z, n_x = mesh.shape["seq"] // 2, mesh.shape["head"] // 2
    fine = Mesh(
        mesh.devices.reshape(n_z, 2, n_x, 2, mesh.shape["dp"]), ("z", "y_hi", "x", "core", "dp")
    )
    tokens, width = ("dp", "z", "y_hi"), ("x", "core")
    wide = P(tokens, width)
    gates = P(("dp", "x", "core"))
    return jax.shard_map(
        functools.partial(per_device, (n_z, n_x)),
        mesh=fine,
        in_specs=(wide,) * 8 + (P(width, None), gates, gates),
        out_specs=(wide, wide),
        check_vma=False,
    )
```

```python
import functools

import jax
import jax.numpy as jnp
from jax import lax
from jax.experimental import pallas as pl
from jax.experimental.pallas import tpu as pltpu
from jax.sharding import Mesh
from jax.sharding import PartitionSpec as P

HD = 128
SCALE = HD ** (-0.5)
SCALE2 = SCALE * 1.4426950408889634
NT = (((1,), (1,)), ((), ()))
BF16 = jnp.bfloat16
F32 = jnp.float32
STATS = 8


def spec_whole():
    return pl.BlockSpec(memory_space=pltpu.VMEM)


def params(mib=12):
    return pltpu.CompilerParams(vmem_limit_bytes=mib * 1024 * 1024)


def query_kernel(q, qt, out, sems):
    copies = []
    for h in range(q.shape[1] // HD):
        for i, ref in enumerate((qt, q)):
            copies.append(
                pltpu.make_async_copy(
                    ref.at[:, h * HD : (h + 1) * HD],
                    out.at[:, (2 * h + i) * HD : (2 * h + i + 1) * HD],
                    sems.at[2 * h + i],
                )
            )
    for copy in copies:
        copy.start()
    for copy in copies:
        copy.wait()


def pack_queries(q, qt):
    rows, width = q.shape
    return pl.pallas_call(
        query_kernel,
        out_shape=jax.ShapeDtypeStruct((rows, 2 * width), BF16),
        in_specs=[pl.BlockSpec(memory_space=pltpu.HBM)] * 2,
        out_specs=spec_whole(),
        scratch_shapes=[pltpu.SemaphoreType.DMA((2 * width // HD,))],
        compiler_params=params(),
        cost_estimate=pl.CostEstimate(flops=0, bytes_accessed=8 * rows * width, transcendentals=0),
        name="pack_queries",
    )(q, qt)


def pack_kernel(k, kt, v, vt, out, scratch, sems):
    heads = k.shape[1] // HD
    values = [
        pltpu.make_async_copy(ref, scratch.at[i], sems.at[2 * heads + i])
        for i, ref in enumerate((v, vt))
    ]
    copies = []
    for h in range(heads):
        for i, ref in enumerate((k, kt)):
            copies.append(
                pltpu.make_async_copy(
                    ref.at[:, h * HD : (h + 1) * HD],
                    out.at[0, 2 * h * HD : 2 * (h + 1) * HD, i * HD : (i + 1) * HD],
                    sems.at[2 * h + i],
                )
            )
    for copy in values + copies:
        copy.start()
    for i, copy in enumerate(values):
        copy.wait()
        for h in range(heads):
            part = scratch[i, :, h * HD : (h + 1) * HD].T
            out[1, (2 * h + i) * HD : (2 * h + i + 1) * HD, :] = part
    for copy in copies:
        copy.wait()


def pack(k, kt, v, vt):
    rows, width = k.shape
    return pl.pallas_call(
        pack_kernel,
        out_shape=jax.ShapeDtypeStruct((2, 2 * width, rows), BF16),
        in_specs=[pl.BlockSpec(memory_space=pltpu.HBM)] * 4,
        out_specs=spec_whole(),
        scratch_shapes=[
            pltpu.VMEM((2, rows, width), BF16),
            pltpu.SemaphoreType.DMA((2 * width // HD + 2,)),
        ],
        compiler_params=params(),
        cost_estimate=pl.CostEstimate(flops=0, bytes_accessed=16 * rows * width, transcendentals=0),
        name="pack",
    )(k, kt, v, vt)


def three_parts(value):
    high = value.astype(BF16)
    rest = value - high.astype(F32)
    middle = rest.astype(BF16)
    low = (rest - middle.astype(F32)).astype(BF16)
    return [high, middle, low]


def attend_kernel(kinds, groups, with_state, final, *refs):
    refs = list(refs)
    scores_ref = refs.pop()
    q_refs = [refs.pop(0), refs.pop(0)]
    pairs = []
    for halves in kinds:
        if halves:
            pairs.append((refs.pop(0), refs.pop(0)))
        else:
            both = refs.pop(0)
            pairs.append((both.at[0], both.at[1]))
    state = refs.pop(0) if with_state else None
    keys = q_refs[0].shape[0]
    tall, far_tall = 2 * HD + STATS, 2 * HD + 2 * STATS
    where = [(g, i) for g, (_, count) in enumerate(groups) for i in range(count)]
    for h, (group, inner) in enumerate(where):
        place = pl.ds(2 * h * HD, 2 * HD)
        q2 = jnp.concatenate([r[:, place] for r in q_refs], axis=0)
        old = state.at[pl.ds(h * tall, tall), :] if with_state else None
        sums = attend_blocks(
            q2, [(k.at[place, :], v.at[place, :]) for k, v in pairs], old, scores_ref
        )
        acc_out, acc_tan, top, total, mixed_sum = sums
        if not final:
            put(refs[0], h * tall, *sums)
            continue
        inverse = 1.0 / total
        ratio = mixed_sum * inverse
        attention = acc_out * inverse
        attention_t = acc_tan * inverse - ratio * attention
        parts = (attention, attention_t, top, total, ratio)
        own, far = refs[0], refs[1 + group]
        put(own, h * tall, *(p[:, :keys] for p in parts))
        base = inner * far_tall
        far[base : base + HD, :] = attention[:, keys:].astype(BF16)
        far[base + HD : base + 2 * HD, :] = attention_t[:, keys:].astype(BF16)
        stats = three_parts(top) + three_parts(total) + three_parts(ratio)
        stats = [s[:, keys:].astype(F32) for s in stats]
        stats.append(jnp.zeros((2 * STATS - len(stats), keys), F32))
        far[base + 2 * HD : base + far_tall, :] = jnp.concatenate(stats, axis=0).astype(BF16)


def put(out, base, upper, lower, *lines):
    out[base : base + HD, :] = upper
    out[base + HD : base + 2 * HD, :] = lower
    for i, line in enumerate(lines):
        out[base + 2 * HD + i : base + 2 * HD + i + 1, :] = line


def attend_blocks(q2, pairs, state, scores_ref):
    rows = q2.shape[0]
    keys = rows // 2
    q = q2[:, HD:]
    top = state[2 * HD : 2 * HD + 1, :] if state is not None else None
    old_top = top
    for i, (k_ref, _) in enumerate(pairs):
        scores = lax.dot_general(k_ref[:, 0:HD], q, NT, preferred_element_type=F32)
        scores_ref[i * keys : (i + 1) * keys, :] = scores
        peak = jnp.max(scores, axis=0, keepdims=True) * SCALE2
        top = peak if top is None else jnp.maximum(top, peak)
    total = jnp.zeros((1, rows), F32)
    mixed_sum = jnp.zeros((1, rows), F32)
    all_weights, all_mixed = [], []
    for i, (k_ref, _) in enumerate(pairs):
        tangent = lax.dot_general(k_ref[...], q2, NT, preferred_element_type=F32)
        weights = jnp.exp2(scores_ref[i * keys : (i + 1) * keys, :] * SCALE2 - top)
        mixed = weights * tangent
        total = total + jnp.sum(weights, axis=0, keepdims=True)
        mixed_sum = mixed_sum + jnp.sum(mixed, axis=0, keepdims=True)
        all_weights.append(weights.astype(BF16))
        all_mixed.append(mixed.astype(BF16))
    values = jnp.concatenate([v_ref[...] for _, v_ref in pairs], axis=1)
    acc = jnp.dot(values, jnp.concatenate(all_weights, axis=0), preferred_element_type=F32)
    acc_mixed = jnp.dot(
        values[0:HD, :], jnp.concatenate(all_mixed, axis=0), preferred_element_type=F32
    )
    acc_out = acc[0:HD, :]
    acc_tan = acc[HD:, :] + SCALE * acc_mixed
    mixed_sum = SCALE * mixed_sum
    if state is not None:
        shrink = jnp.exp2(old_top - top)
        acc_out = acc_out + shrink * state[0:HD, :]
        acc_tan = acc_tan + shrink * state[HD : 2 * HD, :]
        total = total + shrink * state[2 * HD + 1 : 2 * HD + 2, :]
        mixed_sum = mixed_sum + shrink * state[2 * HD + 2 : 2 * HD + 3, :]
    return acc_out, acc_tan, top, total, mixed_sum


def attend(q_own, q_far, groups, blocks, state=None, final=False):
    rows = q_own.shape[0]
    heads = sum(count for _, count in groups)
    n = len(blocks)
    tall, far = 2 * HD + STATS, 2 * HD + 2 * STATS
    kinds = [isinstance(block, tuple) for block in blocks]
    arrays = [q_own, q_far]
    for block in blocks:
        arrays.extend(block if isinstance(block, tuple) else (block,))
    if state is not None:
        arrays.append(state)
    if final:
        outs = [
            jax.ShapeDtypeStruct((heads * tall, rows), F32),
            *(jax.ShapeDtypeStruct((count * far, rows), BF16) for _, count in groups),
        ]
    else:
        outs = [jax.ShapeDtypeStruct((heads * tall, 2 * rows), F32)]
    result = pl.pallas_call(
        functools.partial(attend_kernel, kinds, groups, state is not None, final),
        out_shape=outs,
        in_specs=[spec_whole()] * len(arrays),
        out_specs=[spec_whole()] * len(outs),
        scratch_shapes=[pltpu.VMEM((n * rows, 2 * rows), F32)],
        compiler_params=params(8),
        cost_estimate=pl.CostEstimate(
            flops=4 * heads * 2 * 2 * rows * n * rows * HD * 8,
            bytes_accessed=heads * 2 * rows * HD * 4 * (n + 2),
            transcendentals=heads * 2 * rows * n * rows,
        ),
        name="attend",
    )(*arrays)
    return result if final else result[0]


def merge_kernel(first, own_ref, far_ref, out):
    rows = own_ref.shape[1]
    tall, far_tall = 2 * HD + STATS, 2 * HD + 2 * STATS
    for h in range(far_ref.shape[0] // far_tall):
        own = own_ref[(first + h) * tall : (first + h + 1) * tall, :]
        far = far_ref[h * far_tall : (h + 1) * far_tall, :]
        attention, tangent = merge_parts(own, far)
        out[0:rows, h * HD : (h + 1) * HD] = attention.T.astype(BF16)
        out[rows:, h * HD : (h + 1) * HD] = tangent.T.astype(BF16)


def merge_parts(own, far):
    stats = far[2 * HD :, :].astype(F32)
    pick = lambda i: stats[3 * i : 3 * i + 1] + stats[3 * i + 1 : 3 * i + 2] + stats[3 * i + 2 : 3 * i + 3]
    top0, total0, ratio0 = (own[2 * HD + i : 2 * HD + i + 1, :] for i in range(3))
    top1, total1, ratio1 = pick(0), pick(1), pick(2)
    top = jnp.maximum(top0, top1)
    part0 = total0 * jnp.exp2(top0 - top)
    part1 = total1 * jnp.exp2(top1 - top)
    inverse = 1.0 / (part0 + part1)
    part0, part1 = part0 * inverse, part1 * inverse
    att0, att1 = own[0:HD, :], far[0:HD, :].astype(F32)
    tan0, tan1 = own[HD : 2 * HD, :], far[HD : 2 * HD, :].astype(F32)
    attention = part0 * att0 + part1 * att1
    tangent = part0 * tan0 + part1 * tan1 + (part0 * part1 * (ratio0 - ratio1)) * (att0 - att1)
    return attention, tangent


def merge(first, heads, own, far, cost):
    rows = own.shape[1]
    return pl.pallas_call(
        functools.partial(merge_kernel, first),
        out_shape=jax.ShapeDtypeStruct((2 * rows, heads * HD), BF16),
        in_specs=[spec_whole()] * 2,
        out_specs=spec_whole(),
        compiler_params=params(),
        cost_estimate=pl.CostEstimate(
            flops=cost, bytes_accessed=heads * rows * HD * 14, transcendentals=0
        ),
        name="merge",
    )(own, far)


def stage_kernel(groups, place, weight, *refs):
    count = (len(refs) - 1 - len(groups)) + 1
    pieces, outs, sems = refs[: count - 1], refs[count - 1 : -1], refs[-1]
    width = outs[0].shape[1] // 2
    copies = []
    for (first, heads), out in zip(groups, outs):
        tall = heads * HD
        for d in range(count):
            for half in range(2):
                start = lax.rem(place[1] + half, 2) * width
                if d == 0:
                    start = start + place[0] * (2 * width)
                source = pieces[d - 1] if d else weight
                copies.append(
                    pltpu.make_async_copy(
                        source.at[
                            pl.ds(first * HD, tall), pl.ds(pl.multiple_of(start, HD), width)
                        ],
                        out.at[pl.ds(d * tall, tall), pl.ds(half * width, width)],
                        sems.at[len(copies)],
                    )
                )
    for copy in copies:
        copy.start()
    for copy in copies:
        copy.wait()


def stage(groups, place, weight, pieces):
    depth, width = pieces[0].shape
    count = len(pieces) + 1
    return pl.pallas_call(
        functools.partial(stage_kernel, groups),
        out_shape=[jax.ShapeDtypeStruct((count * n * HD, width), BF16) for _, n in groups],
        in_specs=[pl.BlockSpec(memory_space=pltpu.SMEM)]
        + [pl.BlockSpec(memory_space=pl.ANY)] * count,
        out_specs=[spec_whole()] * len(groups),
        scratch_shapes=[pltpu.SemaphoreType.DMA((2 * count * len(groups),))],
        compiler_params=params(),
        cost_estimate=pl.CostEstimate(
            flops=0, bytes_accessed=4 * count * depth * width, transcendentals=0
        ),
        name="stage",
    )(place, weight, *pieces)


def project_kernel(halves, with_acc, *refs):
    refs = list(refs)
    out = refs.pop()
    acc = refs.pop() if with_acc else None
    weight = refs.pop()
    width = weight.shape[1] // 2
    step = width // 2
    left = jnp.concatenate([r[...] for r in refs], axis=1)
    for i, half in enumerate(halves):
        for j in range(2):
            columns = slice(half * width + j * step, half * width + (j + 1) * step)
            total = jnp.dot(left, weight[:, columns], preferred_element_type=F32)
            if with_acc:
                total = total + acc[:, columns]
            to = i * width + j * step
            out[:, to : to + step] = total.astype(out.dtype)


def project(atts, weight, halves, acc, dtype, cost=0):
    rows = atts[0].shape[0]
    depth, width = weight.shape[0], len(halves) * weight.shape[1] // 2
    arrays = [*atts, weight] + ([] if acc is None else [acc])
    return pl.pallas_call(
        functools.partial(project_kernel, halves, acc is not None),
        out_shape=jax.ShapeDtypeStruct((rows, width), dtype),
        in_specs=[spec_whole()] * len(arrays),
        out_specs=spec_whole(),
        compiler_params=params(16),
        cost_estimate=pl.CostEstimate(
            flops=max(cost, rows * width * depth),
            bytes_accessed=width * (rows * 6 + depth * 2),
            transcendentals=0,
        ),
        name="project",
    )(*arrays)


def finish_kernel(mine, other, res, res_t, gate, gate_t, out, out_t, block, block_t, sems):
    rows = res.shape[0]
    projected = mine[0:rows, :] + other[0:rows, :].astype(F32)
    g = gate[...]
    block[...] = (res[...].astype(F32) + g * projected).astype(block.dtype)
    first = pltpu.make_async_copy(block, out, sems.at[0])
    first.start()
    projected_t = mine[rows:, :] + other[rows:, :].astype(F32)
    block_t[...] = (res_t[...].astype(F32) + gate_t[...] * projected + g * projected_t).astype(
        block_t.dtype
    )
    second = pltpu.make_async_copy(block_t, out_t, sems.at[1])
    second.start()
    first.wait()
    second.wait()


def finish(mine, other, res, res_t, gate, gate_t):
    rows, width = res.shape
    return pl.pallas_call(
        finish_kernel,
        out_shape=[jax.ShapeDtypeStruct((rows, width), BF16)] * 2,
        in_specs=[spec_whole()] * 6,
        out_specs=[pl.BlockSpec(memory_space=pltpu.HBM)] * 2,
        scratch_shapes=[
            pltpu.VMEM((rows, width), BF16),
            pltpu.VMEM((rows, width), BF16),
            pltpu.SemaphoreType.DMA((2,)),
        ],
        compiler_params=params(),
        cost_estimate=pl.CostEstimate(flops=0, bytes_accessed=rows * width * 20, transcendentals=0),
        name="finish",
    )(mine, other, res, res_t, gate[None, :], gate_t[None, :])


def in_hbm(value):
    return pltpu.with_memory_space_constraint(value, pltpu.HBM)


def ring_pairs(size, shift):
    return [(i, (i + shift) % size) for i in range(size)]


def after(value, *others):
    return lax.optimization_barrier((value, others))[0]


def each(values, *others):
    return tuple(after(value, *others) for value in values)


def per_device(sizes, q, qt, k, kt, v, vt, residual, residual_t, weight, gate, gate_t):
    n_z, n_x = sizes
    heads = q.shape[1] // HD
    features = residual.shape[1]
    groups = [(0, heads - 1), (heads - 1, 1)]
    swap = [(0, 1), (1, 0)]
    up, down = ring_pairs(n_z, 1), ring_pairs(n_z, -1)
    q, qt, k, kt, v, vt = (in_hbm(item) for item in (q, qt, k, kt, v, vt))
    packed = pack(k, kt, v, vt)
    q_own = pack_queries(q, qt)
    q_far = lax.ppermute(q_own, "y_hi", swap)

    x = lax.axis_index("x")
    here = jnp.stack([x, lax.axis_index("core")]).astype(jnp.int32)

    def piece(d, *others):
        corner = lax.rem(x + d, n_x) * (2 * features)
        part = lax.dynamic_slice_in_dim(weight, corner, 2 * features, 1)
        return lax.ppermute(after(part, *others), "x", ring_pairs(n_x, d))

    near = [piece(1), piece(n_x - 1)]

    def hop(pair):
        return lax.ppermute(pair[0], "z", up), lax.ppermute(pair[1], "z", down)

    def turn(pair):
        return hop((pair[0][0], pair[1][1]))

    run = functools.partial(attend, q_own, q_far, groups)
    step1 = hop((packed, packed))
    step2 = hop(each(step1, q_far))
    state = run([packed, *step1])
    step3 = hop(each(step2, state, *near))
    state = run([*step2], state=state)
    far_pieces = [piece(d, *near, state) for d in range(2, n_x - 1)]
    pieces = [near[0], *far_pieces, near[1]]
    step4 = turn(each(step3, state))
    state = run([*step3], state=state)
    own, *far = run([step4], state=state, final=True)
    arrived = [
        lax.ppermute(far[0], "y_hi", swap),
        lax.ppermute(after(far[1], far_pieces), "y_hi", swap),
    ]
    gathered = []
    for group, item in zip(groups, arrived):
        att = merge(*group, own, item, 10**10 if group[0] else 0)
        gathered.append(
            [att] + [lax.ppermute(att, "x", ring_pairs(n_x, d)) for d in range(1, n_x)]
        )
    staged = stage(groups, here, in_hbm(weight), [in_hbm(item) for item in after(pieces, att)])
    acc = project(gathered[0], staged[0], (0, 1), None, F32, 10**10)
    run = functools.partial(project, gathered[1], staged[1])
    to_core = run((1,), acc, BF16)
    from_core = lax.ppermute(to_core, "core", swap)
    mine = run((0,), acc, F32)
    return tuple(finish(mine, from_core, residual, residual_t, gate, gate_t))


def solution(mesh):
    n_z, n_x = mesh.shape["seq"] // 2, mesh.shape["head"] // 2
    fine = Mesh(
        mesh.devices.reshape(n_z, 2, n_x, 2, mesh.shape["dp"]), ("z", "y_hi", "x", "core", "dp")
    )
    tokens, width = ("dp", "z", "y_hi"), ("x", "core")
    wide = P(tokens, width)
    gates = P(("dp", "x", "core"))
    return jax.shard_map(
        functools.partial(per_device, (n_z, n_x)),
        mesh=fine,
        in_specs=(wide,) * 8 + (P(width, None), gates, gates),
        out_specs=(wide, wide),
        check_vma=False,
    )
```
